256 devices in a mesh: dp: 64 (over x, z, core), chan: 4 (over y).
Axes of the slice: x: 4, y: 4, z: 8, core: 2. Of those that a mesh axis runs over, the one named last changes fastest.
Arguments:
- activations: bfloat16 [640, 262144], P('chan', 'dp'), may hold values from -6 to 6
- out_grad: bfloat16 [640, 262144], P('chan', 'dp'), may hold values from -6 to 6
- kernel: bfloat16 [640, 5760], P('chan'), may hold values from -0.078125 to 0.078125
- error_in: float32 [64, 640, 5760], P('dp', 'chan'), may hold values from -6 to 6
- q_prev: float32 [640, 4], P('chan'), may hold values from -6 to 6
Outputs:
- in_grad: bfloat16 [640, 262144], P('chan', 'dp')
- q_factor: float32 [640, 4], P('chan')
- new_error: float32 [64, 640, 5760], P('dp', 'chan')
The draws below stay inside these ranges and needn't reach their ends.
All inputs are finite; a program needn't handle non-finite values.
Results may differ from the reference program's by a relative error of at most 0.001.
Values may be sent and summed in bfloat16 or wider, within the bound.
No kernel may reach another device: no remote copies, remote signals or barrier semaphores. Data moves between devices by JAX's collectives and lax.ppermute only.
A program may use at most 128 MiB of HBM per device.

```python
import jax
import jax.numpy as jnp
from jax import lax

C = 640
LAT = 64
RANK = 4
CELLS = 262144
N_DP = 64


def steps_of(own_key, shape, cuts, smallest, largest):
    def one(axis_at, blocks):
        steps = jax.random.uniform(jax.random.fold_in(jax.random.fold_in(own_key, 6), axis_at), (blocks,), jnp.float32, smallest / len(cuts), largest / len(cuts))
        return jnp.repeat(jnp.exp(steps), shape[axis_at] // blocks).reshape((-1,) + (1,) * (len(shape) - axis_at - 1))

    factor_of = one(*cuts[0])
    for cut in cuts[1:]:
        factor_of = factor_of * one(*cut)
    return factor_of


def gaussian(rng, shape, scale, limit, pieces=(), kind=jnp.bfloat16):
    loudness = steps_of(rng, shape, pieces, -0.22, 0.18) if pieces else 1.0
    array = jax.random.normal(rng, shape, jnp.float32) * scale * loudness
    return jnp.minimum(jnp.maximum(array, -limit), limit).astype(kind)


def setup_inputs(seed: int = 0) -> dict:
    keys = jax.random.split(jax.random.key(seed), 6)
    activations = gaussian(keys[0], (C, CELLS), 1.0, 6.0, ((0, 4), (1, 64)))
    out_grad = gaussian(keys[1], (C, CELLS), 1.0, 6.0, ((0, 4), (1, 64)))
    kernel = gaussian(keys[2], (C, 9 * C), (9 * C) ** -0.5, 0.078125, ((0, 4),))
    error_in = gaussian(keys[3], (N_DP, C, 9 * C), 0.5, 6.0, ((0, 64), (1, 4)), jnp.float32)
    q_prev = gaussian(keys[4], (C, RANK), 1.0, 6.0, ((0, 4),), jnp.float32)
    return {"activations": activations, "out_grad": out_grad, "kernel": kernel, "error_in": error_in, "q_prev": q_prev}


def reference(activations, out_grad, kernel, error_in, q_prev):
    hi = lax.Precision.HIGHEST
    act_cells = activations.T
    grad_cells = out_grad.T
    kernel_taps = kernel.reshape(C, 9, C)
    x_pad = jnp.pad(act_cells.reshape(N_DP, LAT, LAT, C), ((0, 0), (1, 1), (1, 1), (0, 0)))
    g_pad = jnp.pad(grad_cells.reshape(N_DP, LAT, LAT, C), ((0, 0), (1, 1), (1, 1), (0, 0)))

    def shard_grad(index):
        zero = jnp.zeros((), jnp.int32)
        x_rows = lax.dynamic_slice(x_pad, (index.astype(jnp.int32), zero, zero, zero), (1, LAT + 2, LAT + 2, C))[0]
        g_rows = lax.dynamic_slice_in_dim(grad_cells, (index * LAT * LAT).astype(jnp.int32), LAT * LAT, 0)
        tap_terms = []
        for tap_index in range(9):
            row_shift, col_shift = divmod(tap_index, 3)
            window = x_rows[row_shift:row_shift + LAT, col_shift:col_shift + LAT].reshape(-1, C)
            tap_terms.append(lax.dot_general(g_rows.astype(jnp.float32), window.astype(jnp.float32), (((0,), (0,)), ((), ())), preferred_element_type=jnp.float32))
        grad_w = jnp.stack(tap_terms, axis=1) * (1.0 / LAT)
        return grad_w.reshape(C, 9 * C) + error_in[index]
    matrices = lax.map(shard_grad, jnp.arange(N_DP, dtype=jnp.int32))
    sketch = jnp.einsum('icm,cr->mr', matrices, q_prev, precision=hi) / N_DP
    gram = jnp.dot(sketch.T, sketch, precision=hi)
    lower = jnp.linalg.cholesky(gram)
    basis = jax.scipy.linalg.solve_triangular(lower, sketch.T, lower=True).T
    q_factor = jnp.einsum('icm,mr->cr', matrices, basis, precision=hi) / N_DP
    new_error = matrices - jnp.dot(q_factor, basis.T, precision=hi)[None]

    def image_grad(g_image):
        total = jnp.zeros((LAT * LAT, C), jnp.float32)
        for tap_index in range(9):
            row_shift, col_shift = divmod(tap_index, 3)
            window = g_image[2 - row_shift:2 - row_shift + LAT, 2 - col_shift:2 - col_shift + LAT].reshape(-1, C)
            total = total + lax.dot_general(window.astype(jnp.float32), kernel_taps[:, tap_index, :].astype(jnp.float32), (((1,), (0,)), ((), ())), preferred_element_type=jnp.float32)
        return total.astype(jnp.bfloat16)
    in_grad = lax.map(image_grad, g_pad).reshape(N_DP * LAT * LAT, C).T
    return (in_grad, q_factor, new_error)
```

```python
import functools

import jax
import jax.numpy as jnp
from jax import lax
from jax.experimental import pallas as pl
from jax.experimental.pallas import tpu as pltpu
from jax.sharding import PartitionSpec as P

LAT = 64
CELLS = LAT * LAT
TAPS = 9
F32 = jnp.float32
BF16 = jnp.bfloat16
NT = (((1,), (1,)), ((), ()))
NN = (((1,), (0,)), ((), ()))
HI = lax.Precision.HIGHEST


def tap(t):
    return t // 3 - 1, t % 3 - 1


def dot(a, b, dims):
    return lax.dot_general(a, b, dims, preferred_element_type=F32)


def split3(v):
    hi = v.astype(BF16).astype(F32)
    rest = v - hi
    mid = rest.astype(BF16).astype(F32)
    return jnp.concatenate([hi, mid, rest - mid], axis=0).astype(BF16)


def lanes(shape):
    return lax.broadcasted_iota(jnp.int32, shape, 1)


def moved(v, t, sign=1):
    da, db = (sign * d for d in tap(t))
    off = da * LAT + db
    if off == 0:
        return v
    cell = lanes(v.shape)
    row, col = cell >> 6, cell & 63
    ok = None
    if da == 1:
        ok = row >= 1
    elif da == -1:
        ok = row < LAT - 1
    if db:
        inside = col >= 1 if db == 1 else col < LAT - 1
        ok = inside if ok is None else ok & inside
    return jnp.where(ok, pltpu.roll(v, off % CELLS, 1), 0.0)


def upper(v):
    return lax.broadcasted_iota(jnp.int32, v.shape, 0) % 8 < 4


def fold(v8):
    half = CELLS // 2
    return jnp.where(upper(v8[:, :half]), v8[:, :half], v8[:, half:])


def unfold(f):
    other = pltpu.roll(f, 4, 0)
    up = upper(f)
    return jnp.concatenate([jnp.where(up, f, other), jnp.where(up, other, f)], axis=1)


FOLD = CELLS // 2
GROUPS = 5
PAY = FOLD + GROUPS * 256


def ungroup(ref, start, ch):
    return jnp.concatenate([ref[:, start + 256 * i : start + 256 * i + ch] for i in range(GROUPS)], axis=0)


def start_kernel(j_ref, q_ref, qt_ref, g_ref, e_ref, o0, o1, o2, o3, qb, rows, blocks):
    ch = g_ref.shape[0]
    j = j_ref[0]
    y3 = dot(split3(qt_ref[...]), g_ref[...], NN)
    y8 = y3[0:8] + y3[8:16] + y3[16:24]
    y = fold(y8)
    for r in range(4):
        qb[r] = jnp.broadcast_to(q_ref[:, r : r + 1], (ch, 128))
    rows[...] = jnp.zeros_like(rows)
    for t in range(TAPS):
        for v in range(5):
            at = t * 640 + v * 128
            acc = [jnp.zeros((8, 128), F32) for _ in range(4)]
            for c in range(0, ch, 8):
                e = e_ref[c : c + 8, at : at + 128]
                for r in range(4):
                    acc[r] = acc[r] + e * qb[r, c : c + 8, :]
            for r in range(4):
                rows[t * 4 + r : t * 4 + r + 1, v * 128 : (v + 1) * 128] = jnp.sum(acc[r], axis=0, keepdims=True)
    for k in range(4):
        r640 = rows[...]
        if k:
            r640 = pltpu.roll(r640, 640 - k * ch, 1)
        for i in range(GROUPS):
            blocks[k, :, 256 * i : 256 * (i + 1)] = r640[8 * i : 8 * i + 8, :256]
    for s, out in enumerate((o0, o1, o2, o3)):
        out[:, :FOLD] = y
        out[:, FOLD:] = blocks[lax.rem(j + s, 4)]


def sketch_kernel(own, r1, r2, r3, x_ref, out, stack):
    ch = x_ref.shape[0]
    total = own[...] + r1[...] + r2[...] + r3[...]
    y8 = unfold(total[:, :FOLD])
    up = upper(y8)
    for i in range(GROUPS):
        second = moved(y8, 2 * i + 1) if 2 * i + 1 < TAPS else jnp.zeros_like(y8)
        stack[8 * i : 8 * i + 8, :] = jnp.where(up, moved(y8, 2 * i), second)
    c3 = dot(split3(stack[...]), x_ref[...], NT)
    c = (c3[0:40] + c3[40:80] + c3[80:120]) * (1.0 / LAT)
    out[...] = jnp.zeros_like(out)
    for i in range(GROUPS):
        at = 256 * i
        out[:, at : at + ch] = c[8 * i : 8 * i + 8] + total[:, FOLD + at : FOLD + at + ch]


def image_kernel(scale, s_ref, x_ref, out, taps):
    ch = x_ref.shape[0]
    sk = s_ref[...] * scale
    m = jnp.concatenate([sk[:, 256 * i : 256 * i + ch] for i in range(GROUPS)], axis=0)
    u3 = dot(split3(m), x_ref[...], NN)
    taps[...] = u3[0:40] + u3[40:80] + u3[80:120]
    z8 = jnp.zeros((8, CELLS), F32)
    up = upper(z8)
    for i in range(GROUPS):
        u = taps[8 * i : 8 * i + 8, :]
        second = moved(u, 2 * i + 1, -1) if 2 * i + 1 < TAPS else jnp.zeros_like(u)
        z8 = z8 + jnp.where(up, moved(u, 2 * i, -1), second)
    z8 = z8 + pltpu.roll(z8, 4, 0)
    out[:, :FOLD] = fold(z8)
    out[:, FOLD:] = sk


def forward_substitution(low, rows):
    done = []
    for r in range(4):
        v = rows[r]
        for s in range(r):
            v = v - low[r][s] * done[s]
        done.append(v / low[r][r])
    return done


def factor_kernel(j_ref, own, r1, r2, r3, e_ref, g_ref, basis_ref, q_out, blocks, by_rank, acc_ref):
    ch = g_ref.shape[0]
    j = j_ref[0]
    for s, ref in enumerate((own, r1, r2, r3)):
        blocks[lax.rem(j + 4 - s, 4)] = ref[...]
    z8 = unfold(blocks[0, :, :FOLD] + blocks[1, :, :FOLD] + blocks[2, :, :FOLD] + blocks[3, :, :FOLD])
    wide = jnp.zeros((40, 640), F32)
    lane = lanes((40, 640))
    for k in range(4):
        b = jnp.concatenate([blocks[k, :, FOLD + 256 * i : FOLD + 256 * (i + 1)] for i in range(GROUPS)], axis=0)
        b = jnp.concatenate([b, jnp.zeros((40, 384), F32)], axis=1)
        if k:
            b = pltpu.roll(b, k * ch, 1)
        wide = jnp.where((lane >= k * ch) & (lane < (k + 1) * ch), b, wide)
    by_rank[...] = jnp.zeros_like(by_rank)
    for t in range(TAPS):
        for r in range(4):
            by_rank[r, t : t + 1, :] = wide[t * 4 + r : t * 4 + r + 1]
    rows = [by_rank[r] for r in range(4)]
    low = [[None] * 4 for _ in range(4)]
    for r in range(4):
        for s in range(r + 1):
            v = jnp.sum(rows[r] * rows[s], keepdims=True)
            for k in range(s):
                v = v - low[r][k] * low[s][k]
            low[r][s] = jnp.sqrt(v) if r == s else v / low[s][s]
    basis = forward_substitution(low, rows)
    for r in range(4):
        basis_ref[r * 16 : (r + 1) * 16, :] = basis[r]
    z = forward_substitution(low, [z8[r : r + 1] for r in range(4)])
    z = jnp.concatenate(z + [jnp.zeros((4, CELLS), F32)], axis=0)
    q3 = dot(split3(z), g_ref[...], NT)
    q = (q3[0:8] + q3[8:16] + q3[16:24]) * (1.0 / LAT)
    for c0 in range(0, ch, 32):
        acc = [[jnp.zeros((8, 128), F32) for _ in range(4)] for _ in range(4)]
        for t in range(TAPS):
            for v in range(5):
                at = t * 640 + v * 128
                es = [e_ref[c0 + 8 * i : c0 + 8 * i + 8, at : at + 128] for i in range(4)]
                for r in range(4):
                    b = jnp.broadcast_to(basis_ref[r * 16 + t : r * 16 + t + 1, v * 128 : (v + 1) * 128], (8, 128))
                    for i in range(4):
                        acc[i][r] = acc[i][r] + es[i] * b
        for i in range(4):
            for r in range(4):
                acc_ref[r, c0 + 8 * i : c0 + 8 * i + 8, :] = acc[i][r]
    ones = jnp.ones((8, 128), F32)
    row = lax.broadcasted_iota(jnp.int32, q.shape, 0)
    for r in range(4):
        part = lax.dot_general(ones, acc_ref[r], NT, precision=HI, preferred_element_type=F32)
        q = jnp.where(row == r, q + part, q)
    q_out[...] = q


def weight_kernel(j_ref, x0, x1, x3, x2a, x2b, g_ref, e_ref, out, stack, xs, acc):
    ch = g_ref.shape[0]
    j = j_ref[0]

    def place(ref, s, first):
        at = pl.multiple_of(lax.rem(j + 4 - s, 4) * ch + first, 16)
        xs[pl.ds(at, ref.shape[0]), :] = ref[...]

    place(x0, 0, 0)
    place(x1, 1, 0)
    place(x3, 3, 0)
    place(x2a, 2, 0)
    place(x2b, 2, ch // 2)

    def shifted(i, carry):
        at = pl.multiple_of(i * 16, 16)
        g = g_ref[pl.ds(at, 16), :].astype(F32)
        for t in range(TAPS):
            stack[pl.ds(t * ch + at, 16), :] = moved(g, t).astype(BF16)
        return carry

    lax.fori_loop(0, ch // 16, shifted, 0)
    step = 1024
    acc[...] = dot(stack[:, :step], xs[:, :step], NT)

    def more(i, carry):
        cells = pl.ds(pl.multiple_of(i * step, step), step)
        acc[...] += dot(stack[:, cells], xs[:, cells], NT)
        return carry

    lax.fori_loop(1, CELLS // step, more, 0)
    for t in range(TAPS):
        cols = slice(t * 640, (t + 1) * 640)
        out[:, cols] = acc[t * ch : (t + 1) * ch, :] * (1.0 / LAT) + e_ref[:, cols]


def spread(u_ref, i):
    at = pl.multiple_of(i * 8, 8)
    ch = u_ref.shape[0] // TAPS
    total = None
    for t in range(TAPS):
        v = moved(u_ref[pl.ds(t * ch + at, 8), :], t)
        total = v if total is None else total + v
    return pl.ds(at, 8), total


def input_kernel(pairs, *refs):
    ks, gs = refs[:pairs], refs[pairs : 2 * pairs]
    out, u_ref = refs[2 * pairs], refs[2 * pairs + 1]
    step = 512

    def products(i, carry):
        cells = pl.ds(pl.multiple_of(i * step, step), step)
        total = None
        for k, g in zip(ks, gs, strict=True):
            p = dot(k[...], g[:, cells], NN)
            total = p if total is None else total + p
        u_ref[:, cells] = total
        return carry

    lax.fori_loop(0, CELLS // step, products, 0)

    def collect(i, carry):
        rows, total = spread(u_ref, i)
        out[rows, :] = total
        return carry

    lax.fori_loop(0, out.shape[0] // 8, collect, 0)


def last_kernel(k_ref, ga, gb, acc_ref, out, u_ref, g_all):
    half = ga.shape[0]
    g_all[:half, :] = ga[...]
    g_all[half:, :] = gb[...]
    step = 512

    def products(i, carry):
        cells = pl.ds(pl.multiple_of(i * step, step), step)
        u_ref[:, cells] = dot(k_ref[...], g_all[:, cells], NN)
        return carry

    lax.fori_loop(0, CELLS // step, products, 0)

    def collect(i, carry):
        at = pl.multiple_of(i * 16, 16)
        _, first = spread(u_ref, 2 * i)
        _, second = spread(u_ref, 2 * i + 1)
        rows = pl.ds(at, 16)
        out[rows, :] = (jnp.concatenate([first, second], axis=0) + acc_ref[rows, :]).astype(BF16)
        return carry

    lax.fori_loop(0, out.shape[0] // 16, collect, 0)


def error_kernel(n_ref, q_ref, b_ref, out):
    q = [q_ref[:, r : r + 1] for r in range(4)]
    for t in range(TAPS):
        cols = slice(t * 640, (t + 1) * 640)
        v = n_ref[:, cols]
        for r in range(4):
            v = v - q[r] * b_ref[r * 16 + t : r * 16 + t + 1, :]
        out[:, cols] = v


def call(kernel, out_shape, scratch=(), scalars=0, inputs=0, limit=60, **kw):
    whole = pl.BlockSpec(memory_space=pltpu.VMEM)
    scalar = pl.BlockSpec(memory_space=pltpu.SMEM)
    return pl.pallas_call(
        kernel,
        out_shape=out_shape,
        in_specs=[scalar] * scalars + [whole] * inputs,
        out_specs=jax.tree.map(lambda _: whole, out_shape),
        scratch_shapes=list(scratch),
        compiler_params=pltpu.CompilerParams(vmem_limit_bytes=limit << 20),
        **kw,
    )


def around(array, s):
    return lax.ppermute(array, "chan", [(i, (i + s) % 4) for i in range(4)])


def ring(block):
    half = block.shape[0] // 2
    left, right = around(block, 1), around(block, 3)
    return left, right, around(left[:half], 1), around(right[half:], 3)


def summed(array, workers):
    mask = 1
    while mask < workers:
        array = array + lax.ppermute(array, "dp", [(i, i ^ mask) for i in range(workers)])
        mask *= 2
    return array


def per_device(x, g, kernel, error_in, q_prev):
    ch = x.shape[0]
    workers = lax.axis_size("dp")
    j = lax.axis_index("chan").astype(jnp.int32)
    core = lax.axis_index("dp") % 2
    js = j.reshape(1)
    err = error_in[0]
    sds = jax.ShapeDtypeStruct

    xl, xr, xa, xb = ring(x)

    qt = q_prev.T
    pay = sds((8, PAY), F32)
    sent = call(
        start_kernel,
        [pay] * 4,
        [pltpu.VMEM((4, ch, 128), F32), pltpu.VMEM((40, 640), F32), pltpu.VMEM((4, 8, GROUPS * 256), F32)],
        1,
        4,
        16,
    )(js, q_prev, jnp.concatenate([qt, qt], axis=0), g, err)
    got = [around(sent[s], s) for s in (1, 2, 3)]
    part = call(sketch_kernel, sds((8, GROUPS * 256), F32), [pltpu.VMEM((40, CELLS), F32)], 0, 5, 16)(sent[0], *got, x)
    total = summed(part, workers)
    mine = call(functools.partial(image_kernel, 1.0 / workers), pay, [pltpu.VMEM((40, CELLS), F32)], 0, 2, 16)(total, x)
    theirs = [around(mine, s) for s in (1, 2, 3)]
    basis, q_part = call(
        factor_kernel,
        [sds((64, 640), F32), sds((8, ch), F32)],
        [pltpu.VMEM((4, 8, PAY), F32), pltpu.VMEM((4, 16, 640), F32), pltpu.VMEM((4, ch, 128), F32)],
        1,
        6,
        16,
    )(js, mine, *theirs, err, g)
    q_factor = summed(q_part, workers)[:4].T * (1.0 / workers)

    gl, gr, ga, gb = ring(g)

    kt = kernel.T.reshape(TAPS, 4, ch, ch)
    blocks = [lax.dynamic_index_in_dim(kt, (j + s) % 4, 1, False).reshape(TAPS * ch, ch) for s in range(4)]
    rows = TAPS * ch // 2
    halves = jnp.stack([around(lax.dynamic_slice_in_dim(blocks[s], core * rows, rows, 0), s) for s in (1, 2, 3)])
    others = lax.ppermute(halves, "dp", [(i, i ^ 1) for i in range(workers)])
    first, second = jnp.where(core == 0, halves, others), jnp.where(core == 0, others, halves)
    k_all = jnp.concatenate([first, second], axis=1)

    matrix = call(
        weight_kernel,
        sds((ch, TAPS * 640), F32),
        [pltpu.VMEM((TAPS * ch, CELLS), BF16), pltpu.VMEM((4 * ch, CELLS), BF16), pltpu.VMEM((TAPS * ch, 640), F32)],
        1,
        7,
        44,
    )(js, x, xl, xr, xa, xb, g, err)

    acc = call(
        functools.partial(input_kernel, 3), sds((ch, CELLS), F32), [pltpu.VMEM((TAPS * ch, CELLS), F32)], 0, 6, 44
    )(blocks[0], k_all[0], k_all[2], g, gl, gr)
    in_grad = call(
        last_kernel, sds((ch, CELLS), BF16), [pltpu.VMEM((TAPS * ch, CELLS), F32), pltpu.VMEM((ch, CELLS), BF16)], 0, 4, 44
    )(k_all[1], ga, gb, acc)

    n_rows = 32
    new_error = pl.pallas_call(
        error_kernel,
        grid=(ch // n_rows,),
        in_specs=[
            pl.BlockSpec((n_rows, TAPS * 640), lambda i: (i, 0)),
            pl.BlockSpec((n_rows, 4), lambda i: (i, 0)),
            pl.BlockSpec((64, 640), lambda i: (0, 0)),
        ],
        out_specs=pl.BlockSpec((n_rows, TAPS * 640), lambda i: (i, 0)),
        out_shape=sds((ch, TAPS * 640), F32),
        compiler_params=pltpu.CompilerParams(vmem_limit_bytes=16 << 20),
    )(matrix, q_factor, basis)
    return in_grad, q_factor, new_error[None]


def solution(mesh):
    in_specs = (
        P("chan", "dp"),
        P("chan", "dp"),
        P("chan", None),
        P("dp", "chan", None),
        P("chan", None),
    )
    out_specs = (P("chan", "dp"), P("chan", None), P("dp", "chan", None))
    return jax.shard_map(
        per_device, mesh=mesh, in_specs=in_specs, out_specs=out_specs, check_vma=False
    )
```

```python
import functools

import jax
import jax.numpy as jnp
from jax import lax
from jax.experimental import pallas as pl
from jax.experimental.pallas import tpu as pltpu
from jax.sharding import PartitionSpec as P

LAT = 64
CELLS = LAT * LAT
TAPS = 9
F32 = jnp.float32
BF16 = jnp.bfloat16
NT = (((1,), (1,)), ((), ()))
NN = (((1,), (0,)), ((), ()))
HI = lax.Precision.HIGHEST
ROLLED = BF16


def tap(t):
    return t // 3 - 1, t % 3 - 1


def dot(a, b, dims):
    return lax.dot_general(a, b, dims, preferred_element_type=F32)


def split3(v):
    hi = v.astype(BF16).astype(F32)
    rest = v - hi
    mid = rest.astype(BF16).astype(F32)
    return jnp.concatenate([hi, mid, rest - mid], axis=0).astype(BF16)


def lanes(shape):
    return lax.broadcasted_iota(jnp.int32, shape, 1)


def moved(v, t, sign=1):
    da, db = (sign * d for d in tap(t))
    off = da * LAT + db
    if off == 0:
        return v
    cell = lanes(v.shape)
    row, col = cell >> 6, cell & 63
    ok = None
    if da == 1:
        ok = row >= 1
    elif da == -1:
        ok = row < LAT - 1
    if db:
        inside = col >= 1 if db == 1 else col < LAT - 1
        ok = inside if ok is None else ok & inside
    return jnp.where(ok, pltpu.roll(v, off % CELLS, 1), 0.0)


def upper(v):
    return lax.broadcasted_iota(jnp.int32, v.shape, 0) % 8 < 4


def fold(v8):
    half = CELLS // 2
    return jnp.where(upper(v8[:, :half]), v8[:, :half], v8[:, half:])


def unfold(f):
    other = pltpu.roll(f, 4, 0)
    up = upper(f)
    return jnp.concatenate([jnp.where(up, f, other), jnp.where(up, other, f)], axis=1)


FOLD = CELLS // 2
GROUPS = 5
PAY = FOLD + GROUPS * 256


def ungroup(ref, start, ch):
    return jnp.concatenate([ref[:, start + 256 * i : start + 256 * i + ch] for i in range(GROUPS)], axis=0)


def start_kernel(j_ref, q_ref, qt_ref, g_ref, e_ref, o0, o1, o2, o3, qb, rows, blocks):
    ch = g_ref.shape[0]
    j = j_ref[0]
    y3 = dot(split3(qt_ref[...]), g_ref[...], NN)
    y8 = y3[0:8] + y3[8:16] + y3[16:24]
    y = fold(y8)
    for r in range(4):
        qb[r] = jnp.broadcast_to(q_ref[:, r : r + 1], (ch, 128))
    rows[...] = jnp.zeros_like(rows)
    for t in range(TAPS):
        for v in range(5):
            at = t * 640 + v * 128
            acc = [jnp.zeros((8, 128), F32) for _ in range(4)]
            for c in range(0, ch, 8):
                e = e_ref[c : c + 8, at : at + 128]
                for r in range(4):
                    acc[r] = acc[r] + e * qb[r, c : c + 8, :]
            for r in range(4):
                rows[t * 4 + r : t * 4 + r + 1, v * 128 : (v + 1) * 128] = jnp.sum(acc[r], axis=0, keepdims=True)
    for k in range(4):
        r640 = rows[...]
        if k:
            r640 = pltpu.roll(r640, 640 - k * ch, 1)
        for i in range(GROUPS):
            blocks[k, :, 256 * i : 256 * (i + 1)] = r640[8 * i : 8 * i + 8, :256]
    for s, out in enumerate((o0, o1, o2, o3)):
        out[:, :FOLD] = y
        out[:, FOLD:] = blocks[lax.rem(j + s, 4)]


def sketch_kernel(own, r1, r2, r3, x_ref, out, stack):
    ch = x_ref.shape[0]
    total = own[...] + r1[...] + r2[...] + r3[...]
    y8 = unfold(total[:, :FOLD])
    up = upper(y8)
    for i in range(GROUPS):
        second = moved(y8, 2 * i + 1) if 2 * i + 1 < TAPS else jnp.zeros_like(y8)
        stack[8 * i : 8 * i + 8, :] = jnp.where(up, moved(y8, 2 * i), second)
    c3 = dot(split3(stack[...]), x_ref[...], NT)
    c = (c3[0:40] + c3[40:80] + c3[80:120]) * (1.0 / LAT)
    out[...] = jnp.zeros_like(out)
    for i in range(GROUPS):
        at = 256 * i
        out[:, at : at + ch] = c[8 * i : 8 * i + 8] + total[:, FOLD + at : FOLD + at + ch]


def image_kernel(scale, s_ref, x_ref, out, taps):
    ch = x_ref.shape[0]
    sk = s_ref[...] * scale
    m = jnp.concatenate([sk[:, 256 * i : 256 * i + ch] for i in range(GROUPS)], axis=0)
    u3 = dot(split3(m), x_ref[...], NN)
    taps[...] = u3[0:40] + u3[40:80] + u3[80:120]
    z8 = jnp.zeros((8, CELLS), F32)
    up = upper(z8)
    for i in range(GROUPS):
        u = taps[8 * i : 8 * i + 8, :]
        second = moved(u, 2 * i + 1, -1) if 2 * i + 1 < TAPS else jnp.zeros_like(u)
        z8 = z8 + jnp.where(up, moved(u, 2 * i, -1), second)
    z8 = z8 + pltpu.roll(z8, 4, 0)
    out[:, :FOLD] = fold(z8)
    out[:, FOLD:] = sk


def forward_substitution(low, rows):
    done = []
    for r in range(4):
        v = rows[r]
        for s in range(r):
            v = v - low[r][s] * done[s]
        done.append(v / low[r][r])
    return done


def factor_kernel(j_ref, own, r1, r2, r3, e_ref, g_ref, basis_ref, q_out, blocks, by_rank, acc_ref):
    ch = g_ref.shape[0]
    j = j_ref[0]
    for s, ref in enumerate((own, r1, r2, r3)):
        blocks[lax.rem(j + 4 - s, 4)] = ref[...]
    z8 = unfold(blocks[0, :, :FOLD] + blocks[1, :, :FOLD] + blocks[2, :, :FOLD] + blocks[3, :, :FOLD])
    wide = jnp.zeros((40, 640), F32)
    lane = lanes((40, 640))
    for k in range(4):
        b = jnp.concatenate([blocks[k, :, FOLD + 256 * i : FOLD + 256 * (i + 1)] for i in range(GROUPS)], axis=0)
        b = jnp.concatenate([b, jnp.zeros((40, 384), F32)], axis=1)
        if k:
            b = pltpu.roll(b, k * ch, 1)
        wide = jnp.where((lane >= k * ch) & (lane < (k + 1) * ch), b, wide)
    by_rank[...] = jnp.zeros_like(by_rank)
    for t in range(TAPS):
        for r in range(4):
            by_rank[r, t : t + 1, :] = wide[t * 4 + r : t * 4 + r + 1]
    rows = [by_rank[r] for r in range(4)]
    low = [[None] * 4 for _ in range(4)]
    for r in range(4):
        for s in range(r + 1):
            v = jnp.sum(rows[r] * rows[s], keepdims=True)
            for k in range(s):
                v = v - low[r][k] * low[s][k]
            low[r][s] = jnp.sqrt(v) if r == s else v / low[s][s]
    basis = forward_substitution(low, rows)
    for r in range(4):
        basis_ref[r * 16 : (r + 1) * 16, :] = basis[r]
    z = forward_substitution(low, [z8[r : r + 1] for r in range(4)])
    z = jnp.concatenate(z + [jnp.zeros((4, CELLS), F32)], axis=0)
    q3 = dot(split3(z), g_ref[...], NT)
    q = (q3[0:8] + q3[8:16] + q3[16:24]) * (1.0 / LAT)
    for c0 in range(0, ch, 32):
        acc = [[jnp.zeros((8, 128), F32) for _ in range(4)] for _ in range(4)]
        for t in range(TAPS):
            for v in range(5):
                at = t * 640 + v * 128
                es = [e_ref[c0 + 8 * i : c0 + 8 * i + 8, at : at + 128] for i in range(4)]
                for r in range(4):
                    b = jnp.broadcast_to(basis_ref[r * 16 + t : r * 16 + t + 1, v * 128 : (v + 1) * 128], (8, 128))
                    for i in range(4):
                        acc[i][r] = acc[i][r] + es[i] * b
        for i in range(4):
            for r in range(4):
                acc_ref[r, c0 + 8 * i : c0 + 8 * i + 8, :] = acc[i][r]
    ones = jnp.ones((8, 128), F32)
    row = lax.broadcasted_iota(jnp.int32, q.shape, 0)
    for r in range(4):
        part = lax.dot_general(ones, acc_ref[r], NT, precision=HI, preferred_element_type=F32)
        q = jnp.where(row == r, q + part, q)
    q_out[...] = q


def cols_moved(v, db):
    if db == 0:
        return v
    col = lanes(v.shape) & 63
    return jnp.where(col >= 1 if db == 1 else col < LAT - 1, pltpu.roll(v, db % CELLS, 1), jnp.zeros((), v.dtype))


def rows_moved(v):
    w = pltpu.roll(v, LAT, 1)
    edge = lanes((v.shape[0], 128))
    none = jnp.zeros((), v.dtype)
    down = jnp.concatenate([jnp.where(edge < LAT, none, w[:, :128]), w[:, 128:]], axis=1)
    up = jnp.concatenate([w[:, 128:], jnp.where(edge < LAT, w[:, :128], none)], axis=1)
    return up, v, down


def weight_kernel(j_ref, x0, xlt, xlb, xrt, xrb, xa, xb, g_ref, e_ref, out, stack, xs, acc):
    ch = g_ref.shape[0]
    half = ch // 2
    j = j_ref[0]
    for ref, s, first in ((x0, 0, 0), (xlt, 1, 0), (xlb, 1, half), (xrt, 3, 0), (xrb, 3, half), (xa, 2, 0), (xb, 2, half)):
        at = pl.multiple_of(lax.rem(j + 4 - s, 4) * ch + first, 16)
        xs[pl.ds(at, ref.shape[0]), :] = ref[...]

    def shifted(i, carry):
        at = pl.multiple_of(i * 16, 16)
        g = g_ref[pl.ds(at, 16), :].astype(F32)
        for b in range(3):
            for a, v in enumerate(rows_moved(cols_moved(g, b - 1).astype(ROLLED))):
                stack[pl.ds((3 * a + b) * ch + at, 16), :] = v.astype(BF16)
        return carry

    lax.fori_loop(0, ch // 16, shifted, 0)
    step = 1024
    acc[...] = dot(stack[:, :step], xs[:, :step], NT)

    def more(i, carry):
        cells = pl.ds(pl.multiple_of(i * step, step), step)
        acc[...] += dot(stack[:, cells], xs[:, cells], NT)
        return carry

    lax.fori_loop(1, CELLS // step, more, 0)
    for t in range(TAPS):
        cols = slice(t * 640, (t + 1) * 640)
        out[:, cols] = acc[t * ch : (t + 1) * ch, :] * (1.0 / LAT) + e_ref[:, cols]


SIDE = 512
PIECE = SIDE // 8


def block_kernel(at_ref, k_ref, own, p1, p2, p3, wide, blocks):
    ch = k_ref.shape[0]
    j, piece = at_ref[0], at_ref[1]
    wide[...] = jnp.zeros_like(wide)
    lane = lanes((ch, 256))
    for k in range(4):
        for a in range(3):
            for b in range(3):
                base, off = divmod(k * ch, 128)
                at = (3 * a + b) * 4 * ch + base * 128
                v = k_ref[:, at : at + 256].astype(F32)
                base, goal = divmod(b * ch, 128)
                if goal != off:
                    v = pltpu.roll(v, (goal - off) % 256, 1)
                rows, cols = slice(a * ch, (a + 1) * ch), slice(base * 128, base * 128 + 256)
                wide[rows, cols] = jnp.where((lane >= goal) & (lane < goal + ch), v, wide[rows, cols])
        blocks[k] = jnp.transpose(wide[...]).astype(BF16)
    own[...] = blocks[j]
    for s, out in ((1, p1), (2, p2), (3, p3)):
        out[...] = blocks[lax.rem(j + s, 4), pl.ds(pl.multiple_of(piece * PIECE, 16), PIECE), :]


def assemble(piece, pieces_ref, s, block):
    for m in range(8):
        at = pl.multiple_of((piece ^ m) * PIECE, 16)
        block[pl.ds(at, PIECE), :] = pieces_ref[m, s - 1]


def rows_stacked(refs, g3, slot):
    ch = sum(ref.shape[0] for ref in refs)
    g3[slot, 3 * ch :, :] = jnp.zeros((SIDE - 3 * ch, CELLS), BF16)
    at = 0
    for ref in refs:
        n = ref.shape[0]

        def body(i, carry, ref=ref, at=at):
            first = pl.multiple_of(i * 16, 16)
            for a, v in enumerate(rows_moved(ref[pl.ds(first, 16), :].astype(ROLLED))):
                g3[slot, pl.ds(a * ch + at + first, 16), :] = v.astype(BF16)
            return carry

        lax.fori_loop(0, n // 16, body, 0)
        at += n


def products(blocks, g3, v_ref):
    step = 512
    used = v_ref.shape[0]

    def body(i, carry):
        cells = pl.ds(pl.multiple_of(i * step, step), step)
        total = None
        for slot, block in enumerate(blocks):
            p = dot(block[:used, :], g3[slot, :, cells], NN)
            total = p if total is None else total + p
        v_ref[:, cells] = total
        return carry

    lax.fori_loop(0, CELLS // step, body, 0)


def collected(v_ref, at, n):
    ch = v_ref.shape[0] // 3
    v = [v_ref[pl.ds(b * ch + at, n), :] for b in range(3)]
    return v[1] + cols_moved(v[0], -1) + cols_moved(v[2], 1)


def input_kernel(at_ref, k_ref, pieces_ref, g, glt, glb, grt, grb, out, far, blocks, g3, v_ref):
    piece = at_ref[1]
    assemble(piece, pieces_ref, 1, blocks.at[0])
    assemble(piece, pieces_ref, 3, blocks.at[1])
    assemble(piece, pieces_ref, 2, far)
    rows_stacked((g,), g3, 0)
    rows_stacked((glt, glb), g3, 1)
    rows_stacked((grt, grb), g3, 2)
    products((k_ref, blocks.at[0], blocks.at[1]), g3, v_ref)

    def body(i, carry):
        at = pl.multiple_of(i * 8, 8)
        out[pl.ds(at, 8), :] = collected(v_ref, at, 8)
        return carry

    lax.fori_loop(0, out.shape[0] // 8, body, 0)


def last_kernel(far, ga, gb, acc_ref, out, g3, v_ref):
    rows_stacked((ga, gb), g3, 0)
    products((far,), g3, v_ref)

    def body(i, carry):
        at = pl.multiple_of(i * 16, 16)
        rows = pl.ds(at, 16)
        out[rows, :] = (collected(v_ref, at, 16) + acc_ref[rows, :]).astype(BF16)
        return carry

    lax.fori_loop(0, out.shape[0] // 16, body, 0)


def cut_kernel(v_ref, top, bottom):
    half = top.shape[0]
    top[...] = v_ref[:half, :]
    bottom[...] = v_ref[half:, :]


def error_kernel(n_ref, q_ref, b_ref, out):
    q = [q_ref[:, r : r + 1] for r in range(4)]
    for t in range(TAPS):
        cols = slice(t * 640, (t + 1) * 640)
        v = n_ref[:, cols]
        for r in range(4):
            v = v - q[r] * b_ref[r * 16 + t : r * 16 + t + 1, :]
        out[:, cols] = v


def call(kernel, out_shape, scratch=(), scalars=0, inputs=0, limit=60, **kw):
    whole = pl.BlockSpec(memory_space=pltpu.VMEM)
    scalar = pl.BlockSpec(memory_space=pltpu.SMEM)
    return pl.pallas_call(
        kernel,
        out_shape=out_shape,
        in_specs=[scalar] * scalars + [whole] * inputs,
        out_specs=jax.tree.map(lambda _: whole, out_shape),
        scratch_shapes=list(scratch),
        compiler_params=pltpu.CompilerParams(vmem_limit_bytes=limit << 20),
        **kw,
    )


def around(array, s):
    return lax.ppermute(array, "chan", [(i, (i + s) % 4) for i in range(4)])


def cut(block):
    half = jax.ShapeDtypeStruct((block.shape[0] // 2, block.shape[1]), block.dtype)
    return call(cut_kernel, [half, half], (), 0, 1, 8)(block)


def after(value, *others):
    return lax.optimization_barrier((value, *others))[0]


def summed(array, workers):
    mask = 1
    while mask < workers:
        array = array + lax.ppermute(array, "dp", [(i, i ^ mask) for i in range(workers)])
        mask *= 2
    return array


def per_device(x, g, kernel, error_in, q_prev):
    ch = x.shape[0]
    workers = lax.axis_size("dp")
    j = lax.axis_index("chan").astype(jnp.int32)
    worker = lax.axis_index("dp").astype(jnp.int32)
    piece = worker // 16 * 2 + worker % 2
    at = jnp.stack([j, piece])
    err = error_in[0]
    sds = jax.ShapeDtypeStruct

    xt, xb = cut(x)
    xlt, xrb = around(xt, 1), around(xb, 3)
    xlb, xrt = around(xb, 1), around(xt, 3)
    xa, xo = around(xlt, 1), around(xrb, 3)

    qt = q_prev.T
    pay = sds((8, PAY), F32)
    sent = call(
        start_kernel,
        [pay] * 4,
        [pltpu.VMEM((4, ch, 128), F32), pltpu.VMEM((40, 640), F32), pltpu.VMEM((4, 8, GROUPS * 256), F32)],
        1,
        4,
        16,
    )(at, q_prev, jnp.concatenate([qt, qt], axis=0), g, err)
    got = [around(sent[s], s) for s in (1, 2, 3)]
    got[0] = after(got[0], xlt, xrb)
    part = call(sketch_kernel, sds((8, GROUPS * 256), F32), [pltpu.VMEM((40, CELLS), F32)], 0, 5, 16)(sent[0], *got, x)
    total = summed(part, workers)
    total = after(total, xlb, xrt)
    mine = call(functools.partial(image_kernel, 1.0 / workers), pay, [pltpu.VMEM((40, CELLS), F32)], 0, 2, 16)(total, x)
    theirs = [around(mine, s) for s in (1, 2, 3)]
    theirs[0] = after(theirs[0], xa, xo)
    basis, q_part = call(
        factor_kernel,
        [sds((64, 640), F32), sds((8, ch), F32)],
        [pltpu.VMEM((4, 8, PAY), F32), pltpu.VMEM((4, 16, 640), F32), pltpu.VMEM((4, ch, 128), F32)],
        1,
        6,
        16,
    )(at, mine, *theirs, err, g)

    gt, gb = cut(g)
    glt, grb = around(gt, 1), around(gb, 3)
    glb, grt = around(gb, 1), around(gt, 3)
    ga, go = around(glt, 1), around(grb, 3)

    q_sum = summed(q_part, workers)
    q_sum = after(q_sum, glt, grb)
    q_factor = q_sum[:4].T * (1.0 / workers)

    square = sds((SIDE, SIDE), BF16)
    k_own, *k_sent = call(
        block_kernel, [square] + [sds((PIECE, SIDE), BF16)] * 3, [pltpu.VMEM((SIDE, SIDE), F32), pltpu.VMEM((4, SIDE, SIDE), BF16)], 1, 1, 16
    )(at, kernel)
    pieces = jnp.stack([around(v, s) for s, v in zip((1, 2, 3), k_sent, strict=True)])[None]
    for mask in (1, 16, 32):
        pieces = jnp.concatenate([pieces, lax.ppermute(pieces, "dp", [(i, i ^ mask) for i in range(workers)])])

    matrix = call(
        weight_kernel,
        sds((ch, TAPS * 640), F32),
        [pltpu.VMEM((TAPS * ch, CELLS), BF16), pltpu.VMEM((4 * ch, CELLS), BF16), pltpu.VMEM((TAPS * ch, 640), F32)],
        1,
        9,
        44,
    )(at, x, xlt, xlb, xrt, xrb, xa, xo, g, err)

    acc, far = call(
        input_kernel,
        [sds((ch, CELLS), F32), square],
        [pltpu.VMEM((2, SIDE, SIDE), BF16), pltpu.VMEM((3, SIDE, CELLS), BF16), pltpu.VMEM((3 * ch, CELLS), F32)],
        1,
        7,
        44,
    )(at, k_own, pieces, g, glt, glb, grt, grb)
    in_grad = call(
        last_kernel, sds((ch, CELLS), BF16), [pltpu.VMEM((1, SIDE, CELLS), BF16), pltpu.VMEM((3 * ch, CELLS), F32)], 0, 4, 24
    )(far, ga, go, acc)

    n_rows = 32
    new_error = pl.pallas_call(
        error_kernel,
        grid=(ch // n_rows,),
        in_specs=[
            pl.BlockSpec((n_rows, TAPS * 640), lambda i: (i, 0)),
            pl.BlockSpec((n_rows, 4), lambda i: (i, 0)),
            pl.BlockSpec((64, 640), lambda i: (0, 0)),
        ],
        out_specs=pl.BlockSpec((n_rows, TAPS * 640), lambda i: (i, 0)),
        out_shape=sds((ch, TAPS * 640), F32),
        compiler_params=pltpu.CompilerParams(vmem_limit_bytes=16 << 20),
    )(matrix, q_factor, basis)
    return in_grad, q_factor, new_error[None]


def solution(mesh):
    in_specs = (
        P("chan", "dp"),
        P("chan", "dp"),
        P("chan", None),
        P("dp", "chan", None),
        P("chan", None),
    )
    out_specs = (P("chan", "dp"), P("chan", None), P("dp", "chan", None))
    return jax.shard_map(
        per_device, mesh=mesh, in_specs=in_specs, out_specs=out_specs, check_vma=False
    )
```

```python
import functools

import jax
import jax.numpy as jnp
from jax import lax
from jax.experimental import pallas as pl
from jax.experimental.pallas import tpu as pltpu
from jax.sharding import PartitionSpec as P

LAT = 64
CELLS = LAT * LAT
TAPS = 9
F32 = jnp.float32
BF16 = jnp.bfloat16
NT = (((1,), (1,)), ((), ()))
NN = (((1,), (0,)), ((), ()))
HI = lax.Precision.HIGHEST
ROLLED = BF16


def tap(t):
    return t // 3 - 1, t % 3 - 1


def dot(a, b, dims):
    return lax.dot_general(a, b, dims, preferred_element_type=F32)


def split3(v):
    hi = v.astype(BF16).astype(F32)
    rest = v - hi
    mid = rest.astype(BF16).astype(F32)
    return jnp.concatenate([hi, mid, rest - mid], axis=0).astype(BF16)


def lanes(shape):
    return lax.broadcasted_iota(jnp.int32, shape, 1)


def moved(v, t, sign=1):
    da, db = (sign * d for d in tap(t))
    off = da * LAT + db
    if off == 0:
        return v
    cell = lanes(v.shape)
    row, col = cell >> 6, cell & 63
    ok = None
    if da == 1:
        ok = row >= 1
    elif da == -1:
        ok = row < LAT - 1
    if db:
        inside = col >= 1 if db == 1 else col < LAT - 1
        ok = inside if ok is None else ok & inside
    return jnp.where(ok, pltpu.roll(v, off % CELLS, 1), 0.0)


def upper(v):
    return lax.broadcasted_iota(jnp.int32, v.shape, 0) % 8 < 4


def fold(v8):
    half = CELLS // 2
    return jnp.where(upper(v8[:, :half]), v8[:, :half], v8[:, half:])


def unfold(f):
    other = pltpu.roll(f, 4, 0)
    up = upper(f)
    return jnp.concatenate([jnp.where(up, f, other), jnp.where(up, other, f)], axis=1)


FOLD = CELLS // 2
GROUPS = 5
PAY = FOLD + GROUPS * 256


def ungroup(ref, start, ch):
    return jnp.concatenate([ref[:, start + 256 * i : start + 256 * i + ch] for i in range(GROUPS)], axis=0)


def start_kernel(j_ref, qt_ref, g_ref, e_ref, o0, o1, o2, o3, qb, rows, blocks, wide):
    ch = g_ref.shape[0]
    j = j_ref[0]
    wide[...] = jnp.zeros_like(wide)
    wide[0:4, :ch] = qt_ref[...]
    wide[4:8, :ch] = qt_ref[...]
    y3 = dot(split3(wide[0:8, :ch]), g_ref[...], NN)
    y8 = y3[0:8] + y3[8:16] + y3[16:24]
    y = fold(y8)
    q = jnp.transpose(wide[...])[:ch, :]
    for r in range(4):
        qb[r] = jnp.broadcast_to(q[:, r : r + 1], (ch, 128))
    rows[...] = jnp.zeros_like(rows)
    for t in range(TAPS):
        for v in range(5):
            at = t * 640 + v * 128
            acc = [jnp.zeros((8, 128), F32) for _ in range(4)]
            for c in range(0, ch, 8):
                e = e_ref[c : c + 8, at : at + 128]
                for r in range(4):
                    acc[r] = acc[r] + e * qb[r, c : c + 8, :]
            for r in range(4):
                rows[t * 4 + r : t * 4 + r + 1, v * 128 : (v + 1) * 128] = jnp.sum(acc[r], axis=0, keepdims=True)
    for k in range(4):
        r640 = rows[...]
        if k:
            r640 = pltpu.roll(r640, 640 - k * ch, 1)
        for i in range(GROUPS):
            blocks[k, :, 256 * i : 256 * (i + 1)] = r640[8 * i : 8 * i + 8, :256]
    for s, out in enumerate((o0, o1, o2, o3)):
        out[:, :FOLD] = y
        out[:, FOLD:] = blocks[lax.rem(j + s, 4)]


def sketch_kernel(own, r1, r2, r3, x_ref, out, stack, rows):
    ch = x_ref.shape[0]
    total = own[...] + r1[...] + r2[...] + r3[...]
    y8 = unfold(total[:, :FOLD])
    up = upper(y8)
    for i in range(GROUPS):
        second = moved(y8, 2 * i + 1) if 2 * i + 1 < TAPS else jnp.zeros_like(y8)
        stack[8 * i : 8 * i + 8, :] = jnp.where(up, moved(y8, 2 * i), second)
    c3 = dot(split3(stack[...]), x_ref[...], NT)
    c = (c3[0:40] + c3[40:80] + c3[80:120]) * (1.0 / LAT)
    rows[...] = jnp.zeros_like(rows)
    for i in range(GROUPS):
        at = 256 * i
        rows[:, at : at + ch] = c[8 * i : 8 * i + 8] + total[:, FOLD + at : FOLD + at + ch]
    for k in range(out.shape[0]):
        out[k] = rows[...]


def total_kernel(got, out):
    total = got[0]
    for k in range(1, got.shape[0]):
        total = total + got[k]
    for k in range(out.shape[0]):
        out[k] = total


def image_kernel(scale, s_ref, x_ref, out, taps):
    ch = x_ref.shape[0]
    sk = s_ref[0]
    for k in range(1, s_ref.shape[0]):
        sk = sk + s_ref[k]
    sk = sk * scale
    m = jnp.concatenate([sk[:, 256 * i : 256 * i + ch] for i in range(GROUPS)], axis=0)
    u3 = dot(split3(m), x_ref[...], NN)
    taps[...] = u3[0:40] + u3[40:80] + u3[80:120]
    z8 = jnp.zeros((8, CELLS), F32)
    up = upper(z8)
    for i in range(GROUPS):
        u = taps[8 * i : 8 * i + 8, :]
        second = moved(u, 2 * i + 1, -1) if 2 * i + 1 < TAPS else jnp.zeros_like(u)
        z8 = z8 + jnp.where(up, moved(u, 2 * i, -1), second)
    z8 = z8 + pltpu.roll(z8, 4, 0)
    folded = fold(z8)
    for k in range(4):
        out[k, :, :FOLD] = folded
        out[k, :, FOLD:] = sk


def forward_substitution(low, rows):
    done = []
    for r in range(4):
        v = rows[r]
        for s in range(r):
            v = v - low[r][s] * done[s]
        done.append(v / low[r][r])
    return done


def factor_kernel(blocks, e_ref, g_ref, basis_ref, q_out, by_rank, acc_ref):
    ch = g_ref.shape[0]
    z8 = unfold(blocks[0, :, :FOLD] + blocks[1, :, :FOLD] + blocks[2, :, :FOLD] + blocks[3, :, :FOLD])
    wide = jnp.zeros((40, 640), F32)
    lane = lanes((40, 640))
    for k in range(4):
        b = jnp.concatenate([blocks[k, :, FOLD + 256 * i : FOLD + 256 * (i + 1)] for i in range(GROUPS)], axis=0)
        b = jnp.concatenate([b, jnp.zeros((40, 384), F32)], axis=1)
        if k:
            b = pltpu.roll(b, k * ch, 1)
        wide = jnp.where((lane >= k * ch) & (lane < (k + 1) * ch), b, wide)
    by_rank[...] = jnp.zeros_like(by_rank)
    for t in range(TAPS):
        for r in range(4):
            by_rank[r, t : t + 1, :] = wide[t * 4 + r : t * 4 + r + 1]
    rows = [by_rank[r] for r in range(4)]
    low = [[None] * 4 for _ in range(4)]
    for r in range(4):
        for s in range(r + 1):
            v = jnp.sum(rows[r] * rows[s], keepdims=True)
            for k in range(s):
                v = v - low[r][k] * low[s][k]
            low[r][s] = jnp.sqrt(v) if r == s else v / low[s][s]
    basis = forward_substitution(low, rows)
    for r in range(4):
        basis_ref[r * 16 : (r + 1) * 16, :] = basis[r]
    z = forward_substitution(low, [z8[r : r + 1] for r in range(4)])
    z = jnp.concatenate(z + [jnp.zeros((4, CELLS), F32)], axis=0)
    q3 = dot(split3(z), g_ref[...], NT)
    q = (q3[0:8] + q3[8:16] + q3[16:24]) * (1.0 / LAT)
    for c0 in range(0, ch, 32):
        acc = [[jnp.zeros((8, 128), F32) for _ in range(4)] for _ in range(4)]
        for t in range(TAPS):
            for v in range(5):
                at = t * 640 + v * 128
                es = [e_ref[c0 + 8 * i : c0 + 8 * i + 8, at : at + 128] for i in range(4)]
                for r in range(4):
                    b = jnp.broadcast_to(basis_ref[r * 16 + t : r * 16 + t + 1, v * 128 : (v + 1) * 128], (8, 128))
                    for i in range(4):
                        acc[i][r] = acc[i][r] + es[i] * b
        for i in range(4):
            for r in range(4):
                acc_ref[r, c0 + 8 * i : c0 + 8 * i + 8, :] = acc[i][r]
    ones = jnp.ones((8, 128), F32)
    row = lax.broadcasted_iota(jnp.int32, q.shape, 0)
    for r in range(4):
        part = lax.dot_general(ones, acc_ref[r], NT, precision=HI, preferred_element_type=F32)
        q = jnp.where(row == r, q + part, q)
    q = jnp.concatenate([q, jnp.zeros((8, 256 - ch), F32)], axis=1)
    q = jnp.where(upper(q[:, :128]), q[:, :128], pltpu.roll(q[:, 128:], 4, 0))
    for k in range(q_out.shape[0]):
        q_out[k] = q


def right_factor(got, wide, ch):
    total = got[0]
    for k in range(1, got.shape[0]):
        total = total + got[k]
    wide[...] = jnp.zeros_like(wide)
    wide[:8, :128] = total
    wide[:8, 128:] = pltpu.roll(total, 4, 0)
    return jnp.transpose(wide[...])[:ch, :4] * (1.0 / got.shape[0])


def cols_moved(v, db):
    if db == 0:
        return v
    col = lanes(v.shape) & 63
    return jnp.where(col >= 1 if db == 1 else col < LAT - 1, pltpu.roll(v, db % CELLS, 1), jnp.zeros((), v.dtype))


def rows_moved(v):
    w = pltpu.roll(v, LAT, 1)
    edge = lanes((v.shape[0], 128))
    none = jnp.zeros((), v.dtype)
    down = jnp.concatenate([jnp.where(edge < LAT, none, w[:, :128]), w[:, 128:]], axis=1)
    up = jnp.concatenate([w[:, 128:], jnp.where(edge < LAT, w[:, :128], none)], axis=1)
    return up, v, down


def weight_kernel(j_ref, x0, xlt, xlb, xrt, xrb, xa, xb, g_ref, e_ref, got, basis_ref, out, q_out, stack, xs, acc, wide):
    ch = g_ref.shape[0]
    half = ch // 2
    j = j_ref[0]
    for ref, s, first in ((x0, 0, 0), (xlt, 1, 0), (xlb, 1, half), (xrt, 3, 0), (xrb, 3, half), (xa, 2, 0), (xb, 2, half)):
        at = pl.multiple_of(lax.rem(j + 4 - s, 4) * ch + first, 16)
        xs[pl.ds(at, ref.shape[0]), :] = ref[...]

    def shifted(i, carry):
        at = pl.multiple_of(i * 16, 16)
        g = g_ref[pl.ds(at, 16), :].astype(F32)
        for b in range(3):
            for a, v in enumerate(rows_moved(cols_moved(g, b - 1).astype(ROLLED))):
                stack[pl.ds((3 * a + b) * ch + at, 16), :] = v.astype(BF16)
        return carry

    lax.fori_loop(0, ch // 16, shifted, 0)
    step = 2048
    acc[...] = dot(stack[:, :step], xs[:, :step], NT)

    def more(i, carry):
        cells = pl.ds(pl.multiple_of(i * step, step), step)
        acc[...] += dot(stack[:, cells], xs[:, cells], NT)
        return carry

    lax.fori_loop(1, CELLS // step, more, 0)
    q_out[...] = right_factor(got, wide, ch)
    for t in range(TAPS):
        for c in range(0, ch, 32):
            rows, cols = slice(c, c + 32), slice(t * 640, (t + 1) * 640)
            v = acc[t * ch + c : t * ch + c + 32, :] * (1.0 / LAT) + e_ref[rows, cols]
            for r in range(4):
                v = v - q_out[rows, r : r + 1] * basis_ref[r * 16 + t : r * 16 + t + 1, :]
            out[rows, cols] = v


SIDE = 512
PIECE = SIDE // 2


def block_kernel(at_ref, k_ref, own, p1, p2, p3, wide, blocks):
    ch = k_ref.shape[0]
    j, piece = at_ref[0], at_ref[1]
    wide[...] = jnp.zeros_like(wide)
    lane = lanes((ch, 256))
    for k in range(4):
        for a in range(3):
            for b in range(3):
                base, off = divmod(k * ch, 128)
                at = (3 * a + b) * 4 * ch + base * 128
                v = k_ref[:, at : at + 256].astype(F32)
                base, goal = divmod(b * ch, 128)
                if goal != off:
                    v = pltpu.roll(v, (goal - off) % 256, 1)
                rows, cols = slice(a * ch, (a + 1) * ch), slice(base * 128, base * 128 + 256)
                wide[rows, cols] = jnp.where((lane >= goal) & (lane < goal + ch), v, wide[rows, cols])
        blocks[k] = jnp.transpose(wide[...]).astype(BF16)
    own[...] = blocks[j]
    rows = pl.ds(pl.multiple_of(piece * PIECE, PIECE), PIECE)
    for s, out in ((1, p1), (2, p2), (3, p3)):
        out[...] = blocks[lax.rem(j + s, 4), rows, :]


def rows_stacked(refs, g3, slot):
    ch = sum(ref.shape[0] for ref in refs)
    g3[slot, 3 * ch :, :] = jnp.zeros((SIDE - 3 * ch, CELLS), BF16)
    start = 0
    for ref in refs:

        def body(i, carry, ref=ref, start=start):
            at = pl.multiple_of(i * 16, 16)
            for a, v in enumerate(rows_moved(ref[pl.ds(at, 16), :].astype(ROLLED))):
                g3[slot, pl.ds(a * ch + start + at, 16), :] = v.astype(BF16)
            return carry

        lax.fori_loop(0, ref.shape[0] // 16, body, 0)
        start += ref.shape[0]


def products(blocks, g3, v_ref):
    step = 512
    used = v_ref.shape[0]

    def body(i, carry):
        cells = pl.ds(pl.multiple_of(i * step, step), step)
        total = None
        for slot, block in enumerate(blocks):
            p = dot(block[:used, :], g3[slot, :, cells], NN)
            total = p if total is None else total + p
        v_ref[:, cells] = total
        return carry

    lax.fori_loop(0, CELLS // step, body, 0)


def collected(v_ref, at, n):
    ch = v_ref.shape[0] // 3
    v = [v_ref[pl.ds(b * ch + at, n), :] for b in range(3)]
    return v[1] + cols_moved(v[0], -1) + cols_moved(v[2], 1)


def own_kernel(k_ref, g, out, g3, v_ref):
    rows_stacked((g,), g3, 0)
    products((k_ref,), g3, v_ref)

    def body(i, carry):
        at = pl.multiple_of(i * 16, 16)
        out[pl.ds(at, 16), :] = collected(v_ref, at, 16)
        return carry

    lax.fori_loop(0, out.shape[0] // 16, body, 0)


def rest_kernel(at_ref, mine_ref, other_ref, glt, glb, grt, grb, ga, go, acc_ref, out, blocks, g3, v_ref):
    first = pl.multiple_of(at_ref[1] * PIECE, PIECE)
    second = pl.multiple_of((1 - at_ref[1]) * PIECE, PIECE)
    for s, refs in enumerate(((glt, glb), (ga, go), (grt, grb))):
        blocks[s, pl.ds(first, PIECE), :] = mine_ref[s]
        blocks[s, pl.ds(second, PIECE), :] = other_ref[s]
        rows_stacked(refs, g3, s)
    products([blocks.at[s] for s in range(3)], g3, v_ref)

    def body(i, carry):
        at = pl.multiple_of(i * 16, 16)
        rows = pl.ds(at, 16)
        out[rows, :] = (collected(v_ref, at, 16) + acc_ref[rows, :]).astype(BF16)
        return carry

    lax.fori_loop(0, out.shape[0] // 16, body, 0)


def cut_kernel(v_ref, top, bottom):
    half = top.shape[0]
    top[...] = v_ref[:half, :]
    bottom[...] = v_ref[half:, :]


def call(kernel, out_shape, scratch=(), scalars=0, inputs=0, limit=60, **kw):
    whole = pl.BlockSpec(memory_space=pltpu.VMEM)
    scalar = pl.BlockSpec(memory_space=pltpu.SMEM)
    return pl.pallas_call(
        kernel,
        out_shape=out_shape,
        in_specs=[scalar] * scalars + [whole] * inputs,
        out_specs=jax.tree.map(lambda _: whole, out_shape),
        scratch_shapes=list(scratch),
        compiler_params=pltpu.CompilerParams(vmem_limit_bytes=limit << 20),
        **kw,
    )


def around(array, s):
    return lax.ppermute(array, "chan", [(i, (i + s) % 4) for i in range(4)])


def cut(block):
    half = jax.ShapeDtypeStruct((block.shape[0] // 2, block.shape[1]), block.dtype)
    return call(cut_kernel, [half, half], (), 0, 1, 8)(block)


def after(value, *others):
    return lax.optimization_barrier((value, *others))[0]


def line_groups(axis):
    if axis == "z":
        return [[x * 16 + z * 2 + c for z in range(8)] for x in range(4) for c in range(2)]
    return [[x * 16 + z * 2 + c for x in range(4) for c in range(2)] for z in range(8)]


def exchanged(array, axis):
    return lax.all_to_all(array, "dp", 0, 0, axis_index_groups=line_groups(axis), tiled=True)


def per_device(x, g, kernel, error_in, q_prev):
    ch = x.shape[0]
    workers = lax.axis_size("dp")
    j = lax.axis_index("chan").astype(jnp.int32)
    worker = lax.axis_index("dp").astype(jnp.int32)
    at = jnp.stack([j, worker % 2])
    err = error_in[0]
    sds = jax.ShapeDtypeStruct

    gt, gb = cut(g)
    glt, grb = around(gt, 1), around(gb, 3)

    pay = sds((8, PAY), F32)
    sent = call(
        start_kernel,
        [pay] * 4,
        [
            pltpu.VMEM((4, ch, 128), F32),
            pltpu.VMEM((40, 640), F32),
            pltpu.VMEM((4, 8, GROUPS * 256), F32),
            pltpu.VMEM((128, 256), F32),
        ],
        1,
        3,
        16,
    )(at, q_prev.T, g, err)
    got = [around(sent[s], s) for s in (1, 2, 3)]

    k_own, *k_sent = call(
        block_kernel,
        [sds((SIDE, SIDE), BF16)] + [sds((PIECE, SIDE), BF16)] * 3,
        [pltpu.VMEM((SIDE, SIDE), F32), pltpu.VMEM((4, SIDE, SIDE), BF16)],
        1,
        1,
        16,
    )(at, after(kernel, *sent))
    acc = call(
        own_kernel, sds((ch, CELLS), F32), [pltpu.VMEM((1, SIDE, CELLS), BF16), pltpu.VMEM((3 * ch, CELLS), F32)], 0, 2, 24
    )(k_own, g)
    got[0] = after(got[0], glt, grb, acc)

    group = sds((8, 8, GROUPS * 256), F32)
    part = call(
        sketch_kernel, group, [pltpu.VMEM((40, CELLS), F32), pltpu.VMEM((8, GROUPS * 256), F32)], 0, 5, 16
    )(sent[0], *got, x)
    part, gb, gt = lax.optimization_barrier((part, gb, gt))
    glb, grt = around(gb, 1), around(gt, 3)
    part = exchanged(part, "xc")
    part = call(total_kernel, group, (), 0, 1, 8)(part)
    glt, grb, part = lax.optimization_barrier((glt, grb, part))
    ga, go = around(glt, 1), around(grb, 3)
    part = after(exchanged(part, "z"), glb, grt)
    mine = call(
        functools.partial(image_kernel, 1.0 / workers), sds((4, 8, PAY), F32), [pltpu.VMEM((40, CELLS), F32)], 0, 2, 16
    )(part, x)
    xt, xb = cut(x)
    mine = after(mine, ga, go, xt, xb)
    theirs = lax.all_to_all(mine, "chan", 0, 0, tiled=True)
    xt, xb, theirs, *k_sent = lax.optimization_barrier((xt, xb, theirs, *k_sent))
    xlt, xrb = around(xt, 1), around(xb, 3)
    xlb, xrt = around(xb, 1), around(xt, 3)
    k_got = [around(v, s) for s, v in zip((1, 2, 3), k_sent, strict=True)]
    basis, q_part = call(
        factor_kernel,
        [sds((64, 640), F32), sds((workers, 8, 128), F32)],
        [pltpu.VMEM((4, 16, 640), F32), pltpu.VMEM((4, ch, 128), F32)],
        0,
        3,
        16,
    )(theirs, err, g)
    q_got = lax.all_to_all(q_part, "dp", 0, 0, tiled=True)
    xlt, xrb, q_got, *k_got = lax.optimization_barrier((xlt, xrb, q_got, *k_got))
    k_mine = jnp.stack(k_got)
    k_other = lax.ppermute(k_mine, "dp", [(i, i ^ 1) for i in range(workers)])
    xa, xo = around(xlt, 1), around(xrb, 3)

    in_grad = call(
        rest_kernel,
        sds((ch, CELLS), BF16),
        [pltpu.VMEM((3, SIDE, SIDE), BF16), pltpu.VMEM((3, SIDE, CELLS), BF16), pltpu.VMEM((3 * ch, CELLS), F32)],
        1,
        9,
        44,
    )(after(at, q_got), k_mine, k_other, glt, glb, grt, grb, ga, go, acc)

    new_error, q_factor = call(
        weight_kernel,
        [sds((ch, TAPS * 640), F32), sds((ch, 4), F32)],
        [
            pltpu.VMEM((TAPS * ch, CELLS), BF16),
            pltpu.VMEM((4 * ch, CELLS), BF16),
            pltpu.VMEM((TAPS * ch, 640), F32),
            pltpu.VMEM((128, 256), F32),
        ],
        1,
        11,
        44,
    )(at, x, xlt, xlb, xrt, xrb, xa, xo, g, err, after(q_got, in_grad), basis)
    return in_grad, q_factor, new_error[None]


def solution(mesh):
    in_specs = (
        P("chan", "dp"),
        P("chan", "dp"),
        P("chan", None),
        P("dp", "chan", None),
        P("chan", None),
    )
    out_specs = (P("chan", "dp"), P("chan", None), P("dp", "chan", None))
    return jax.shard_map(
        per_device, mesh=mesh, in_specs=in_specs, out_specs=out_specs, check_vma=False
    )
```

```python
import functools

import jax
import jax.numpy as jnp
from jax import lax
from jax.experimental import pallas as pl
from jax.experimental.pallas import tpu as pltpu
from jax.sharding import PartitionSpec as P

LAT = 64
CELLS = LAT * LAT
TAPS = 9
F32 = jnp.float32
BF16 = jnp.bfloat16
NT = (((1,), (1,)), ((), ()))
NN = (((1,), (0,)), ((), ()))
HI = lax.Precision.HIGHEST
ROLLED = BF16


def tap(t):
    return t // 3 - 1, t % 3 - 1


def dot(a, b, dims):
    return lax.dot_general(a, b, dims, preferred_element_type=F32)


def split3(v):
    hi = v.astype(BF16).astype(F32)
    rest = v - hi
    mid = rest.astype(BF16).astype(F32)
    return jnp.concatenate([hi, mid, rest - mid], axis=0).astype(BF16)


def lanes(shape):
    return lax.broadcasted_iota(jnp.int32, shape, 1)


def moved(v, t, sign=1):
    da, db = (sign * d for d in tap(t))
    off = da * LAT + db
    if off == 0:
        return v
    cell = lanes(v.shape)
    row, col = cell >> 6, cell & 63
    ok = None
    if da == 1:
        ok = row >= 1
    elif da == -1:
        ok = row < LAT - 1
    if db:
        inside = col >= 1 if db == 1 else col < LAT - 1
        ok = inside if ok is None else ok & inside
    return jnp.where(ok, pltpu.roll(v, off % CELLS, 1), 0.0)


def upper(v):
    return lax.broadcasted_iota(jnp.int32, v.shape, 0) % 8 < 4


def fold(v8):
    half = CELLS // 2
    return jnp.where(upper(v8[:, :half]), v8[:, :half], v8[:, half:])


def unfold(f):
    other = pltpu.roll(f, 4, 0)
    up = upper(f)
    return jnp.concatenate([jnp.where(up, f, other), jnp.where(up, other, f)], axis=1)


FOLD = CELLS // 2
GROUPS = 5
PAY = FOLD + GROUPS * 256


def ungroup(ref, start, ch):
    return jnp.concatenate([ref[:, start + 256 * i : start + 256 * i + ch] for i in range(GROUPS)], axis=0)


def start_kernel(j_ref, qt_ref, g_ref, e_ref, o0, o1, o2, o3, qb, rows, blocks, wide):
    ch = g_ref.shape[0]
    j = j_ref[0]
    wide[...] = jnp.zeros_like(wide)
    wide[0:4, :ch] = qt_ref[...]
    wide[4:8, :ch] = qt_ref[...]
    y3 = dot(split3(wide[0:8, :ch]), g_ref[...], NN)
    y8 = y3[0:8] + y3[8:16] + y3[16:24]
    y = fold(y8)
    q = jnp.transpose(wide[...])[:ch, :]
    for r in range(4):
        qb[r] = jnp.broadcast_to(q[:, r : r + 1], (ch, 128))
    rows[...] = jnp.zeros_like(rows)
    for t in range(TAPS):
        for v in range(5):
            at = t * 640 + v * 128
            acc = [jnp.zeros((8, 128), F32) for _ in range(4)]
            for c in range(0, ch, 8):
                e = e_ref[c : c + 8, at : at + 128]
                for r in range(4):
                    acc[r] = acc[r] + e * qb[r, c : c + 8, :]
            for r in range(4):
                rows[t * 4 + r : t * 4 + r + 1, v * 128 : (v + 1) * 128] = jnp.sum(acc[r], axis=0, keepdims=True)
    for k in range(4):
        r640 = rows[...]
        if k:
            r640 = pltpu.roll(r640, 640 - k * ch, 1)
        for i in range(GROUPS):
            blocks[k, :, 256 * i : 256 * (i + 1)] = r640[8 * i : 8 * i + 8, :256]
    for s, out in enumerate((o0, o1, o2, o3)):
        out[:, :FOLD] = y
        out[:, FOLD:] = blocks[lax.rem(j + s, 4)]


def sketch_kernel(own, r1, r2, r3, x_ref, out, stack, rows):
    ch = x_ref.shape[0]
    total = own[...] + r1[...] + r2[...] + r3[...]
    y8 = unfold(total[:, :FOLD])
    up = upper(y8)
    for i in range(GROUPS):
        second = moved(y8, 2 * i + 1) if 2 * i + 1 < TAPS else jnp.zeros_like(y8)
        stack[8 * i : 8 * i + 8, :] = jnp.where(up, moved(y8, 2 * i), second)
    c3 = dot(split3(stack[...]), x_ref[...], NT)
    c = (c3[0:40] + c3[40:80] + c3[80:120]) * (1.0 / LAT)
    rows[...] = jnp.zeros_like(rows)
    for i in range(GROUPS):
        at = 256 * i
        rows[:, at : at + ch] = c[8 * i : 8 * i + 8] + total[:, FOLD + at : FOLD + at + ch]
    for k in range(out.shape[0]):
        out[k] = rows[...]


def total_kernel(got, out):
    total = got[0]
    for k in range(1, got.shape[0]):
        total = total + got[k]
    for k in range(out.shape[0]):
        out[k] = total


def image_kernel(scale, s_ref, x_ref, out, taps):
    ch = x_ref.shape[0]
    sk = s_ref[0]
    for k in range(1, s_ref.shape[0]):
        sk = sk + s_ref[k]
    sk = sk * scale
    m = jnp.concatenate([sk[:, 256 * i : 256 * i + ch] for i in range(GROUPS)], axis=0)
    u3 = dot(split3(m), x_ref[...], NN)
    taps[...] = u3[0:40] + u3[40:80] + u3[80:120]
    z8 = jnp.zeros((8, CELLS), F32)
    up = upper(z8)
    for i in range(GROUPS):
        u = taps[8 * i : 8 * i + 8, :]
        second = moved(u, 2 * i + 1, -1) if 2 * i + 1 < TAPS else jnp.zeros_like(u)
        z8 = z8 + jnp.where(up, moved(u, 2 * i, -1), second)
    z8 = z8 + pltpu.roll(z8, 4, 0)
    folded = fold(z8)
    for k in range(4):
        out[k, :, :FOLD] = folded
        out[k, :, FOLD:] = sk


def forward_substitution(low, rows):
    done = []
    for r in range(4):
        v = rows[r]
        for s in range(r):
            v = v - low[r][s] * done[s]
        done.append(v / low[r][r])
    return done


def factor_kernel(blocks, e_ref, g_ref, basis_ref, q_out, by_rank, acc_ref):
    ch = g_ref.shape[0]
    z8 = unfold(blocks[0, :, :FOLD] + blocks[1, :, :FOLD] + blocks[2, :, :FOLD] + blocks[3, :, :FOLD])
    wide = jnp.zeros((40, 640), F32)
    lane = lanes((40, 640))
    for k in range(4):
        b = jnp.concatenate([blocks[k, :, FOLD + 256 * i : FOLD + 256 * (i + 1)] for i in range(GROUPS)], axis=0)
        b = jnp.concatenate([b, jnp.zeros((40, 384), F32)], axis=1)
        if k:
            b = pltpu.roll(b, k * ch, 1)
        wide = jnp.where((lane >= k * ch) & (lane < (k + 1) * ch), b, wide)
    by_rank[...] = jnp.zeros_like(by_rank)
    for t in range(TAPS):
        for r in range(4):
            by_rank[r, t : t + 1, :] = wide[t * 4 + r : t * 4 + r + 1]
    rows = [by_rank[r] for r in range(4)]
    low = [[None] * 4 for _ in range(4)]
    for r in range(4):
        for s in range(r + 1):
            v = jnp.sum(rows[r] * rows[s], keepdims=True)
            for k in range(s):
                v = v - low[r][k] * low[s][k]
            low[r][s] = jnp.sqrt(v) if r == s else v / low[s][s]
    basis = forward_substitution(low, rows)
    for r in range(4):
        basis_ref[r * 16 : (r + 1) * 16, :] = basis[r]
    z = forward_substitution(low, [z8[r : r + 1] for r in range(4)])
    z = jnp.concatenate(z + [jnp.zeros((4, CELLS), F32)], axis=0)
    q3 = dot(split3(z), g_ref[...], NT)
    q = (q3[0:8] + q3[8:16] + q3[16:24]) * (1.0 / LAT)
    for c0 in range(0, ch, 32):
        acc = [[jnp.zeros((8, 128), F32) for _ in range(4)] for _ in range(4)]
        for t in range(TAPS):
            for v in range(5):
                at = t * 640 + v * 128
                es = [e_ref[c0 + 8 * i : c0 + 8 * i + 8, at : at + 128] for i in range(4)]
                for r in range(4):
                    b = jnp.broadcast_to(basis_ref[r * 16 + t : r * 16 + t + 1, v * 128 : (v + 1) * 128], (8, 128))
                    for i in range(4):
                        acc[i][r] = acc[i][r] + es[i] * b
        for i in range(4):
            for r in range(4):
                acc_ref[r, c0 + 8 * i : c0 + 8 * i + 8, :] = acc[i][r]
    ones = jnp.ones((8, 128), F32)
    row = lax.broadcasted_iota(jnp.int32, q.shape, 0)
    for r in range(4):
        part = lax.dot_general(ones, acc_ref[r], NT, precision=HI, preferred_element_type=F32)
        q = jnp.where(row == r, q + part, q)
    q = jnp.concatenate([q, jnp.zeros((8, 256 - ch), F32)], axis=1)
    q = jnp.where(upper(q[:, :128]), q[:, :128], pltpu.roll(q[:, 128:], 4, 0))
    for k in range(q_out.shape[0]):
        q_out[k] = q


def right_factor(got, wide, ch):
    total = got[0]
    for k in range(1, got.shape[0]):
        total = total + got[k]
    wide[...] = jnp.zeros_like(wide)
    wide[:8, :128] = total
    wide[:8, 128:] = pltpu.roll(total, 4, 0)
    return jnp.transpose(wide[...])[:ch, :4] * (1.0 / got.shape[0])


def cols_moved(v, db):
    if db == 0:
        return v
    col = lanes(v.shape) & 63
    return jnp.where(col >= 1 if db == 1 else col < LAT - 1, pltpu.roll(v, db % CELLS, 1), jnp.zeros((), v.dtype))


def rows_moved(v):
    w = pltpu.roll(v, LAT, 1)
    edge = lanes((v.shape[0], 128))
    none = jnp.zeros((), v.dtype)
    down = jnp.concatenate([jnp.where(edge < LAT, none, w[:, :128]), w[:, 128:]], axis=1)
    up = jnp.concatenate([w[:, 128:], jnp.where(edge < LAT, w[:, :128], none)], axis=1)
    return up, v, down


def weight_kernel(j_ref, x0, xlt, xlb, xrt, xrb, xa, xb, g_ref, e_ref, got, basis_ref, out, q_out, stack, xs, acc, wide):
    ch = g_ref.shape[0]
    half = ch // 2
    j = j_ref[0]
    for ref, s, first in ((x0, 0, 0), (xlt, 1, 0), (xlb, 1, half), (xrt, 3, 0), (xrb, 3, half), (xa, 2, 0), (xb, 2, half)):
        at = pl.multiple_of(lax.rem(j + 4 - s, 4) * ch + first, 16)
        xs[pl.ds(at, ref.shape[0]), :] = ref[...]

    def shifted(i, carry):
        at = pl.multiple_of(i * 16, 16)
        g = g_ref[pl.ds(at, 16), :].astype(F32)
        for b in range(3):
            for a, v in enumerate(rows_moved(cols_moved(g, b - 1).astype(ROLLED))):
                stack[pl.ds((3 * a + b) * ch + at, 16), :] = v.astype(BF16)
        return carry

    lax.fori_loop(0, ch // 16, shifted, 0)
    step = 2048
    acc[...] = dot(stack[:, :step], xs[:, :step], NT)

    def more(i, carry):
        cells = pl.ds(pl.multiple_of(i * step, step), step)
        acc[...] += dot(stack[:, cells], xs[:, cells], NT)
        return carry

    lax.fori_loop(1, CELLS // step, more, 0)
    q_out[...] = right_factor(got, wide, ch)
    for t in range(TAPS):
        for c in range(0, ch, 32):
            rows, cols = slice(c, c + 32), slice(t * 640, (t + 1) * 640)
            v = acc[t * ch + c : t * ch + c + 32, :] * (1.0 / LAT) + e_ref[rows, cols]
            for r in range(4):
                v = v - q_out[rows, r : r + 1] * basis_ref[r * 16 + t : r * 16 + t + 1, :]
            out[rows, cols] = v


SIDE = 512
PIECE = SIDE // 2


def block_kernel(at_ref, k_ref, own, p1, p2, p3, wide, blocks):
    ch = k_ref.shape[0]
    j, piece = at_ref[0], at_ref[1]
    wide[...] = jnp.zeros_like(wide)
    lane = lanes((ch, 256))
    for k in range(4):
        for a in range(3):
            for b in range(3):
                base, off = divmod(k * ch, 128)
                at = (3 * a + b) * 4 * ch + base * 128
                v = k_ref[:, at : at + 256].astype(F32)
                base, goal = divmod(b * ch, 128)
                if goal != off:
                    v = pltpu.roll(v, (goal - off) % 256, 1)
                rows, cols = slice(a * ch, (a + 1) * ch), slice(base * 128, base * 128 + 256)
                wide[rows, cols] = jnp.where((lane >= goal) & (lane < goal + ch), v, wide[rows, cols])
        blocks[k] = jnp.transpose(wide[...]).astype(BF16)
    own[...] = blocks[j]
    rows = pl.ds(pl.multiple_of(piece * PIECE, PIECE), PIECE)
    for s, out in ((1, p1), (2, p2), (3, p3)):
        out[...] = blocks[lax.rem(j + s, 4), rows, :]


def rows_stacked(refs, g3, slot):
    ch = sum(ref.shape[0] for ref in refs)
    g3[slot, 3 * ch :, :] = jnp.zeros((SIDE - 3 * ch, CELLS), BF16)
    start = 0
    for ref in refs:

        def body(i, carry, ref=ref, start=start):
            at = pl.multiple_of(i * 16, 16)
            for a, v in enumerate(rows_moved(ref[pl.ds(at, 16), :].astype(ROLLED))):
                g3[slot, pl.ds(a * ch + start + at, 16), :] = v.astype(BF16)
            return carry

        lax.fori_loop(0, ref.shape[0] // 16, body, 0)
        start += ref.shape[0]


def products(blocks, g3, v_ref):
    step = 512
    used = v_ref.shape[0]

    def body(i, carry):
        cells = pl.ds(pl.multiple_of(i * step, step), step)
        total = None
        for slot, block in enumerate(blocks):
            p = dot(block[:used, :], g3[slot, :, cells], NN)
            total = p if total is None else total + p
        v_ref[:, cells] = total
        return carry

    lax.fori_loop(0, CELLS // step, body, 0)


def collected(v_ref, at, n):
    ch = v_ref.shape[0] // 3
    v = [v_ref[pl.ds(b * ch + at, n), :] for b in range(3)]
    return v[1] + cols_moved(v[0], -1) + cols_moved(v[2], 1)


def own_kernel(k_ref, g, out, g3, v_ref):
    rows_stacked((g,), g3, 0)
    products((k_ref,), g3, v_ref)

    def body(i, carry):
        at = pl.multiple_of(i * 16, 16)
        out[pl.ds(at, 16), :] = collected(v_ref, at, 16)
        return carry

    lax.fori_loop(0, out.shape[0] // 16, body, 0)


def rest_kernel(at_ref, mine_ref, other_ref, glt, glb, grt, grb, ga, go, acc_ref, out, blocks, g3, v_ref):
    first = pl.multiple_of(at_ref[1] * PIECE, PIECE)
    second = pl.multiple_of((1 - at_ref[1]) * PIECE, PIECE)
    for s, refs in enumerate(((glt, glb), (ga, go), (grt, grb))):
        blocks[s, pl.ds(first, PIECE), :] = mine_ref[s]
        blocks[s, pl.ds(second, PIECE), :] = other_ref[s]
        rows_stacked(refs, g3, s)
    products([blocks.at[s] for s in range(3)], g3, v_ref)

    def body(i, carry):
        at = pl.multiple_of(i * 16, 16)
        rows = pl.ds(at, 16)
        out[rows, :] = (collected(v_ref, at, 16) + acc_ref[rows, :]).astype(BF16)
        return carry

    lax.fori_loop(0, out.shape[0] // 16, body, 0)


def cut_kernel(v_ref, top, bottom):
    half = top.shape[0]
    top[...] = v_ref[:half, :]
    bottom[...] = v_ref[half:, :]


def call(kernel, out_shape, scratch=(), scalars=0, inputs=0, limit=60, **kw):
    whole = pl.BlockSpec(memory_space=pltpu.VMEM)
    scalar = pl.BlockSpec(memory_space=pltpu.SMEM)
    return pl.pallas_call(
        kernel,
        out_shape=out_shape,
        in_specs=[scalar] * scalars + [whole] * inputs,
        out_specs=jax.tree.map(lambda _: whole, out_shape),
        scratch_shapes=list(scratch),
        compiler_params=pltpu.CompilerParams(vmem_limit_bytes=limit << 20),
        **kw,
    )


def around(array, s):
    return lax.ppermute(array, "chan", [(i, (i + s) % 4) for i in range(4)])


def cut(block):
    half = jax.ShapeDtypeStruct((block.shape[0] // 2, block.shape[1]), block.dtype)
    return call(cut_kernel, [half, half], (), 0, 1, 8)(block)


def after(value, *others):
    return lax.optimization_barrier((value, *others))[0]


def line_groups(axis):
    if axis == "z":
        return [[x * 16 + z * 2 + c for z in range(8)] for x in range(4) for c in range(2)]
    return [[x * 16 + z * 2 + c for x in range(4) for c in range(2)] for z in range(8)]


def exchanged(array, axis):
    return lax.all_to_all(array, "dp", 0, 0, axis_index_groups=line_groups(axis), tiled=True)


def per_device(x, g, kernel, error_in, q_prev):
    ch = x.shape[0]
    workers = lax.axis_size("dp")
    j = lax.axis_index("chan").astype(jnp.int32)
    worker = lax.axis_index("dp").astype(jnp.int32)
    at = jnp.stack([j, worker % 2])
    err = error_in[0]
    sds = jax.ShapeDtypeStruct

    gt, gb = cut(g)
    glt, grb = around(gt, 1), around(gb, 3)

    pay = sds((8, PAY), F32)
    sent = call(
        start_kernel,
        [pay] * 4,
        [
            pltpu.VMEM((4, ch, 128), F32),
            pltpu.VMEM((40, 640), F32),
            pltpu.VMEM((4, 8, GROUPS * 256), F32),
            pltpu.VMEM((128, 256), F32),
        ],
        1,
        3,
        16,
    )(at, q_prev.T, g, err)
    got = [around(sent[s], s) for s in (1, 2, 3)]

    k_own, *k_sent = call(
        block_kernel,
        [sds((SIDE, SIDE), BF16)] + [sds((PIECE, SIDE), BF16)] * 3,
        [pltpu.VMEM((SIDE, SIDE), F32), pltpu.VMEM((4, SIDE, SIDE), BF16)],
        1,
        1,
        16,
    )(at, after(kernel, *sent))
    acc = call(
        own_kernel, sds((ch, CELLS), F32), [pltpu.VMEM((1, SIDE, CELLS), BF16), pltpu.VMEM((3 * ch, CELLS), F32)], 0, 2, 24
    )(k_own, g)
    got[0] = after(got[0], glt, grb, acc)

    group = sds((8, 8, GROUPS * 256), F32)
    part = call(
        sketch_kernel, group, [pltpu.VMEM((40, CELLS), F32), pltpu.VMEM((8, GROUPS * 256), F32)], 0, 5, 16
    )(sent[0], *got, x)
    part, gb, gt = lax.optimization_barrier((part, gb, gt))
    glb, grt = around(gb, 1), around(gt, 3)
    part = after(exchanged(part, "xc"), glb, grt)
    part = call(total_kernel, group, (), 0, 1, 8)(part)
    glt, grb, part, *k_sent = lax.optimization_barrier((glt, grb, part, *k_sent))
    k_got = [around(v, s) for s, v in zip((1, 2, 3), k_sent, strict=True)]
    ga, go = around(glt, 1), around(grb, 3)
    part = exchanged(part, "z")
    mine = call(
        functools.partial(image_kernel, 1.0 / workers), sds((4, 8, PAY), F32), [pltpu.VMEM((40, CELLS), F32)], 0, 2, 16
    )(part, x)
    xt, xb = cut(x)
    mine, *k_got = lax.optimization_barrier((mine, *k_got, ga, go, xt, xb))[:4]
    k_mine = jnp.stack(k_got)
    k_other = lax.ppermute(k_mine, "dp", [(i, i ^ 1) for i in range(workers)])
    theirs = lax.all_to_all(mine, "chan", 0, 0, tiled=True)
    xt, xb, theirs = lax.optimization_barrier((xt, xb, theirs))
    xlt, xrb = around(xt, 1), around(xb, 3)
    xlb, xrt = around(xb, 1), around(xt, 3)
    basis, q_part = call(
        factor_kernel,
        [sds((64, 640), F32), sds((workers, 8, 128), F32)],
        [pltpu.VMEM((4, 16, 640), F32), pltpu.VMEM((4, ch, 128), F32)],
        0,
        3,
        16,
    )(theirs, err, g)
    q_got = lax.all_to_all(q_part, "dp", 0, 0, tiled=True)
    xlt, xrb, q_got = lax.optimization_barrier((xlt, xrb, q_got))
    xa, xo = around(xlt, 1), around(xrb, 3)

    in_grad = call(
        rest_kernel,
        sds((ch, CELLS), BF16),
        [pltpu.VMEM((3, SIDE, SIDE), BF16), pltpu.VMEM((3, SIDE, CELLS), BF16), pltpu.VMEM((3 * ch, CELLS), F32)],
        1,
        9,
        44,
    )(after(at, q_got), k_mine, k_other, glt, glb, grt, grb, ga, go, acc)

    new_error, q_factor = call(
        weight_kernel,
        [sds((ch, TAPS * 640), F32), sds((ch, 4), F32)],
        [
            pltpu.VMEM((TAPS * ch, CELLS), BF16),
            pltpu.VMEM((4 * ch, CELLS), BF16),
            pltpu.VMEM((TAPS * ch, 640), F32),
            pltpu.VMEM((128, 256), F32),
        ],
        1,
        11,
        44,
    )(at, x, xlt, xlb, xrt, xrb, xa, xo, g, err, after(q_got, in_grad), basis)
    return in_grad, q_factor, new_error[None]


def solution(mesh):
    in_specs = (
        P("chan", "dp"),
        P("chan", "dp"),
        P("chan", None),
        P("dp", "chan", None),
        P("chan", None),
    )
    out_specs = (P("chan", "dp"), P("chan", None), P("dp", "chan", None))
    return jax.shard_map(
        per_device, mesh=mesh, in_specs=in_specs, out_specs=out_specs, check_vma=False
    )
```

```python
import functools

import jax
import jax.numpy as jnp
from jax import lax
from jax.experimental import pallas as pl
from jax.experimental.pallas import tpu as pltpu
from jax.sharding import PartitionSpec as P

LAT = 64
CELLS = LAT * LAT
TAPS = 9
F32 = jnp.float32
BF16 = jnp.bfloat16
NT = (((1,), (1,)), ((), ()))
NN = (((1,), (0,)), ((), ()))
HI = lax.Precision.HIGHEST
ROLLED = BF16


def tap(t):
    return t // 3 - 1, t % 3 - 1


def dot(a, b, dims):
    return lax.dot_general(a, b, dims, preferred_element_type=F32)


def split3(v):
    hi = v.astype(BF16).astype(F32)
    rest = v - hi
    mid = rest.astype(BF16).astype(F32)
    return jnp.concatenate([hi, mid, rest - mid], axis=0).astype(BF16)


def lanes(shape):
    return lax.broadcasted_iota(jnp.int32, shape, 1)


def moved(v, t, sign=1):
    da, db = (sign * d for d in tap(t))
    off = da * LAT + db
    if off == 0:
        return v
    cell = lanes(v.shape)
    row, col = cell >> 6, cell & 63
    ok = None
    if da == 1:
        ok = row >= 1
    elif da == -1:
        ok = row < LAT - 1
    if db:
        inside = col >= 1 if db == 1 else col < LAT - 1
        ok = inside if ok is None else ok & inside
    return jnp.where(ok, pltpu.roll(v, off % CELLS, 1), 0.0)


def upper(v):
    return lax.broadcasted_iota(jnp.int32, v.shape, 0) % 8 < 4


def fold(v8):
    half = CELLS // 2
    return jnp.where(upper(v8[:, :half]), v8[:, :half], v8[:, half:])


def unfold(f):
    other = pltpu.roll(f, 4, 0)
    up = upper(f)
    return jnp.concatenate([jnp.where(up, f, other), jnp.where(up, other, f)], axis=1)


FOLD = CELLS // 2
GROUPS = 5
PAY = FOLD + GROUPS * 256


def ungroup(ref, start, ch):
    return jnp.concatenate([ref[:, start + 256 * i : start + 256 * i + ch] for i in range(GROUPS)], axis=0)


def start_kernel(j_ref, qt_ref, g_ref, e_ref, o0, o1, o2, o3, qb, rows, blocks, wide):
    ch = g_ref.shape[0]
    j = j_ref[0]
    wide[...] = jnp.zeros_like(wide)
    wide[0:4, :ch] = qt_ref[...]
    wide[4:8, :ch] = qt_ref[...]
    y3 = dot(split3(wide[0:8, :ch]), g_ref[...], NN)
    y8 = y3[0:8] + y3[8:16] + y3[16:24]
    y = fold(y8)
    q = jnp.transpose(wide[...])[:ch, :]
    for r in range(4):
        qb[r] = jnp.broadcast_to(q[:, r : r + 1], (ch, 128))
    rows[...] = jnp.zeros_like(rows)
    for t in range(TAPS):
        for v in range(5):
            at = t * 640 + v * 128
            acc = [jnp.zeros((8, 128), F32) for _ in range(4)]
            for c in range(0, ch, 8):
                e = e_ref[c : c + 8, at : at + 128]
                for r in range(4):
                    acc[r] = acc[r] + e * qb[r, c : c + 8, :]
            for r in range(4):
                rows[t * 4 + r : t * 4 + r + 1, v * 128 : (v + 1) * 128] = jnp.sum(acc[r], axis=0, keepdims=True)
    for k in range(4):
        r640 = rows[...]
        if k:
            r640 = pltpu.roll(r640, 640 - k * ch, 1)
        for i in range(GROUPS):
            blocks[k, :, 256 * i : 256 * (i + 1)] = r640[8 * i : 8 * i + 8, :256]
    for s, out in enumerate((o0, o1, o2, o3)):
        out[:, :FOLD] = y
        out[:, FOLD:] = blocks[lax.rem(j + s, 4)]


def sketch_kernel(own, r1, r2, r3, x_ref, out, stack, rows):
    ch = x_ref.shape[0]
    total = own[...] + r1[...] + r2[...] + r3[...]
    y8 = unfold(total[:, :FOLD])
    up = upper(y8)
    for i in range(GROUPS):
        second = moved(y8, 2 * i + 1) if 2 * i + 1 < TAPS else jnp.zeros_like(y8)
        stack[8 * i : 8 * i + 8, :] = jnp.where(up, moved(y8, 2 * i), second)
    c3 = dot(split3(stack[...]), x_ref[...], NT)
    c = (c3[0:40] + c3[40:80] + c3[80:120]) * (1.0 / LAT)
    rows[...] = jnp.zeros_like(rows)
    for i in range(GROUPS):
        at = 256 * i
        rows[:, at : at + ch] = c[8 * i : 8 * i + 8] + total[:, FOLD + at : FOLD + at + ch]
    for k in range(out.shape[0]):
        out[k] = rows[...]


def total_kernel(got, out):
    total = got[0]
    for k in range(1, got.shape[0]):
        total = total + got[k]
    for k in range(out.shape[0]):
        out[k] = total


def image_kernel(scale, s_ref, x_ref, out, taps):
    ch = x_ref.shape[0]
    sk = s_ref[0]
    for k in range(1, s_ref.shape[0]):
        sk = sk + s_ref[k]
    sk = sk * scale
    m = jnp.concatenate([sk[:, 256 * i : 256 * i + ch] for i in range(GROUPS)], axis=0)
    u3 = dot(split3(m), x_ref[...], NN)
    taps[...] = u3[0:40] + u3[40:80] + u3[80:120]
    z8 = jnp.zeros((8, CELLS), F32)
    up = upper(z8)
    for i in range(GROUPS):
        u = taps[8 * i : 8 * i + 8, :]
        second = moved(u, 2 * i + 1, -1) if 2 * i + 1 < TAPS else jnp.zeros_like(u)
        z8 = z8 + jnp.where(up, moved(u, 2 * i, -1), second)
    z8 = z8 + pltpu.roll(z8, 4, 0)
    folded = fold(z8)
    for k in range(4):
        out[k, :, :FOLD] = folded
        out[k, :, FOLD:] = sk


def forward_substitution(low, rows):
    done = []
    for r in range(4):
        v = rows[r]
        for s in range(r):
            v = v - low[r][s] * done[s]
        done.append(v / low[r][r])
    return done


def factor_kernel(blocks, e_ref, g_ref, basis_ref, q_out, by_rank, acc_ref):
    ch = g_ref.shape[0]
    z8 = unfold(blocks[0, :, :FOLD] + blocks[1, :, :FOLD] + blocks[2, :, :FOLD] + blocks[3, :, :FOLD])
    wide = jnp.zeros((40, 640), F32)
    lane = lanes((40, 640))
    for k in range(4):
        b = jnp.concatenate([blocks[k, :, FOLD + 256 * i : FOLD + 256 * (i + 1)] for i in range(GROUPS)], axis=0)
        b = jnp.concatenate([b, jnp.zeros((40, 384), F32)], axis=1)
        if k:
            b = pltpu.roll(b, k * ch, 1)
        wide = jnp.where((lane >= k * ch) & (lane < (k + 1) * ch), b, wide)
    by_rank[...] = jnp.zeros_like(by_rank)
    for t in range(TAPS):
        for r in range(4):
            by_rank[r, t : t + 1, :] = wide[t * 4 + r : t * 4 + r + 1]
    rows = [by_rank[r] for r in range(4)]
    low = [[None] * 4 for _ in range(4)]
    for r in range(4):
        for s in range(r + 1):
            v = jnp.sum(rows[r] * rows[s], keepdims=True)
            for k in range(s):
                v = v - low[r][k] * low[s][k]
            low[r][s] = jnp.sqrt(v) if r == s else v / low[s][s]
    basis = forward_substitution(low, rows)
    for r in range(4):
        basis_ref[r * 16 : (r + 1) * 16, :] = basis[r]
    z = forward_substitution(low, [z8[r : r + 1] for r in range(4)])
    z = jnp.concatenate(z + [jnp.zeros((4, CELLS), F32)], axis=0)
    q3 = dot(split3(z), g_ref[...], NT)
    q = (q3[0:8] + q3[8:16] + q3[16:24]) * (1.0 / LAT)
    for c0 in range(0, ch, 32):
        acc = [[jnp.zeros((8, 128), F32) for _ in range(4)] for _ in range(4)]
        for t in range(TAPS):
            for v in range(5):
                at = t * 640 + v * 128
                es = [e_ref[c0 + 8 * i : c0 + 8 * i + 8, at : at + 128] for i in range(4)]
                for r in range(4):
                    b = jnp.broadcast_to(basis_ref[r * 16 + t : r * 16 + t + 1, v * 128 : (v + 1) * 128], (8, 128))
                    for i in range(4):
                        acc[i][r] = acc[i][r] + es[i] * b
        for i in range(4):
            for r in range(4):
                acc_ref[r, c0 + 8 * i : c0 + 8 * i + 8, :] = acc[i][r]
    ones = jnp.ones((8, 128), F32)
    row = lax.broadcasted_iota(jnp.int32, q.shape, 0)
    for r in range(4):
        part = lax.dot_general(ones, acc_ref[r], NT, precision=HI, preferred_element_type=F32)
        q = jnp.where(row == r, q + part, q)
    q = jnp.concatenate([q, jnp.zeros((8, 256 - ch), F32)], axis=1)
    q = jnp.where(upper(q[:, :128]), q[:, :128], pltpu.roll(q[:, 128:], 4, 0))
    for k in range(q_out.shape[0]):
        q_out[k] = q


def right_factor(got, wide, ch):
    total = got[0]
    for k in range(1, got.shape[0]):
        total = total + got[k]
    wide[...] = jnp.zeros_like(wide)
    wide[:8, :128] = total
    wide[:8, 128:] = pltpu.roll(total, 4, 0)
    return jnp.transpose(wide[...])[:ch, :4] * (1.0 / got.shape[0])


def cols_moved(v, db):
    if db == 0:
        return v
    col = lanes(v.shape) & 63
    return jnp.where(col >= 1 if db == 1 else col < LAT - 1, pltpu.roll(v, db % CELLS, 1), jnp.zeros((), v.dtype))


def rows_moved(v):
    w = pltpu.roll(v, LAT, 1)
    edge = lanes((v.shape[0], 128))
    none = jnp.zeros((), v.dtype)
    down = jnp.concatenate([jnp.where(edge < LAT, none, w[:, :128]), w[:, 128:]], axis=1)
    up = jnp.concatenate([w[:, 128:], jnp.where(edge < LAT, w[:, :128], none)], axis=1)
    return up, v, down


def weight_kernel(j_ref, x0, xlt, xlb, xrt, xrb, xa, xb, g_ref, e_ref, got, basis_ref, out, q_out, stack, xs, acc, wide):
    ch = g_ref.shape[0]
    half = ch // 2
    j = j_ref[0]
    for ref, s, first in ((x0, 0, 0), (xlt, 1, 0), (xlb, 1, half), (xrt, 3, 0), (xrb, 3, half), (xa, 2, 0), (xb, 2, half)):
        at = pl.multiple_of(lax.rem(j + 4 - s, 4) * ch + first, 16)
        xs[pl.ds(at, ref.shape[0]), :] = ref[...]

    def shifted(i, carry):
        at = pl.multiple_of(i * 16, 16)
        g = g_ref[pl.ds(at, 16), :].astype(F32)
        for b in range(3):
            for a, v in enumerate(rows_moved(cols_moved(g, b - 1).astype(ROLLED))):
                stack[pl.ds((3 * a + b) * ch + at, 16), :] = v.astype(BF16)
        return carry

    lax.fori_loop(0, ch // 16, shifted, 0)
    step = 2048
    acc[...] = dot(stack[:, :step], xs[:, :step], NT)

    def more(i, carry):
        cells = pl.ds(pl.multiple_of(i * step, step), step)
        acc[...] += dot(stack[:, cells], xs[:, cells], NT)
        return carry

    lax.fori_loop(1, CELLS // step, more, 0)
    q_out[...] = right_factor(got, wide, ch)
    for t in range(TAPS):
        for c in range(0, ch, 32):
            rows, cols = slice(c, c + 32), slice(t * 640, (t + 1) * 640)
            v = acc[t * ch + c : t * ch + c + 32, :] * (1.0 / LAT) + e_ref[rows, cols]
            for r in range(4):
                v = v - q_out[rows, r : r + 1] * basis_ref[r * 16 + t : r * 16 + t + 1, :]
            out[rows, cols] = v


SIDE = 512
PIECE = SIDE // 2


def block_kernel(at_ref, k_ref, own, p1, p2, p3, wide, blocks):
    ch = k_ref.shape[0]
    j, piece = at_ref[0], at_ref[1]
    wide[...] = jnp.zeros_like(wide)
    lane = lanes((ch, 256))
    for k in range(4):
        for a in range(3):
            for b in range(3):
                base, off = divmod(k * ch, 128)
                at = (3 * a + b) * 4 * ch + base * 128
                v = k_ref[:, at : at + 256].astype(F32)
                base, goal = divmod(b * ch, 128)
                if goal != off:
                    v = pltpu.roll(v, (goal - off) % 256, 1)
                rows, cols = slice(a * ch, (a + 1) * ch), slice(base * 128, base * 128 + 256)
                wide[rows, cols] = jnp.where((lane >= goal) & (lane < goal + ch), v, wide[rows, cols])
        blocks[k] = jnp.transpose(wide[...]).astype(BF16)
    own[...] = blocks[j]
    rows = pl.ds(pl.multiple_of(piece * PIECE, PIECE), PIECE)
    for s, out in ((1, p1), (2, p2), (3, p3)):
        out[...] = blocks[lax.rem(j + s, 4), rows, :]


def rows_stacked(refs, g3, slot):
    ch = sum(ref.shape[0] for ref in refs)
    g3[slot, 3 * ch :, :] = jnp.zeros((SIDE - 3 * ch, CELLS), BF16)
    start = 0
    for ref in refs:

        def body(i, carry, ref=ref, start=start):
            at = pl.multiple_of(i * 16, 16)
            for a, v in enumerate(rows_moved(ref[pl.ds(at, 16), :].astype(ROLLED))):
                g3[slot, pl.ds(a * ch + start + at, 16), :] = v.astype(BF16)
            return carry

        lax.fori_loop(0, ref.shape[0] // 16, body, 0)
        start += ref.shape[0]


def products(blocks, g3, v_ref):
    step = 512
    used = v_ref.shape[0]

    def body(i, carry):
        cells = pl.ds(pl.multiple_of(i * step, step), step)
        total = None
        for slot, block in enumerate(blocks):
            p = dot(block[:used, :], g3[slot, :, cells], NN)
            total = p if total is None else total + p
        v_ref[:, cells] = total
        return carry

    lax.fori_loop(0, CELLS // step, body, 0)


def collected(v_ref, at, n):
    ch = v_ref.shape[0] // 3
    v = [v_ref[pl.ds(b * ch + at, n), :] for b in range(3)]
    return v[1] + cols_moved(v[0], -1) + cols_moved(v[2], 1)


def own_kernel(k_ref, g, out, g3, v_ref):
    rows_stacked((g,), g3, 0)
    products((k_ref,), g3, v_ref)

    def body(i, carry):
        at = pl.multiple_of(i * 16, 16)
        out[pl.ds(at, 16), :] = collected(v_ref, at, 16)
        return carry

    lax.fori_loop(0, out.shape[0] // 16, body, 0)


def rest_kernel(at_ref, mine_ref, other_ref, glt, glb, grt, grb, ga, go, acc_ref, out, blocks, g3, v_ref):
    first = pl.multiple_of(at_ref[1] * PIECE, PIECE)
    second = pl.multiple_of((1 - at_ref[1]) * PIECE, PIECE)
    for s, refs in enumerate(((glt, glb), (ga, go), (grt, grb))):
        blocks[s, pl.ds(first, PIECE), :] = mine_ref[s]
        blocks[s, pl.ds(second, PIECE), :] = other_ref[s]
        rows_stacked(refs, g3, s)
    products([blocks.at[s] for s in range(3)], g3, v_ref)

    def body(i, carry):
        at = pl.multiple_of(i * 16, 16)
        rows = pl.ds(at, 16)
        out[rows, :] = (collected(v_ref, at, 16) + acc_ref[rows, :]).astype(BF16)
        return carry

    lax.fori_loop(0, out.shape[0] // 16, body, 0)


def cut_kernel(v_ref, top, bottom):
    half = top.shape[0]
    top[...] = v_ref[:half, :]
    bottom[...] = v_ref[half:, :]


def call(kernel, out_shape, scratch=(), scalars=0, inputs=0, limit=60, **kw):
    whole = pl.BlockSpec(memory_space=pltpu.VMEM)
    scalar = pl.BlockSpec(memory_space=pltpu.SMEM)
    return pl.pallas_call(
        kernel,
        out_shape=out_shape,
        in_specs=[scalar] * scalars + [whole] * inputs,
        out_specs=jax.tree.map(lambda _: whole, out_shape),
        scratch_shapes=list(scratch),
        compiler_params=pltpu.CompilerParams(vmem_limit_bytes=limit << 20),
        **kw,
    )


def around(array, s):
    return lax.ppermute(array, "chan", [(i, (i + s) % 4) for i in range(4)])


def cut(block):
    half = jax.ShapeDtypeStruct((block.shape[0] // 2, block.shape[1]), block.dtype)
    return call(cut_kernel, [half, half], (), 0, 1, 8)(block)


def after(value, *others):
    return lax.optimization_barrier((value, *others))[0]


def line_groups(axis):
    if axis == "z":
        return [[x * 16 + z * 2 + c for z in range(8)] for x in range(4) for c in range(2)]
    return [[x * 16 + z * 2 + c for x in range(4) for c in range(2)] for z in range(8)]


def exchanged(array, axis):
    return lax.all_to_all(array, "dp", 0, 0, axis_index_groups=line_groups(axis), tiled=True)


def per_device(x, g, kernel, error_in, q_prev):
    ch = x.shape[0]
    workers = lax.axis_size("dp")
    j = lax.axis_index("chan").astype(jnp.int32)
    worker = lax.axis_index("dp").astype(jnp.int32)
    at = jnp.stack([j, worker % 2])
    err = error_in[0]
    sds = jax.ShapeDtypeStruct

    gt, gb = cut(g)
    glt, grb = around(gt, 1), around(gb, 3)

    pay = sds((8, PAY), F32)
    sent = call(
        start_kernel,
        [pay] * 4,
        [
            pltpu.VMEM((4, ch, 128), F32),
            pltpu.VMEM((40, 640), F32),
            pltpu.VMEM((4, 8, GROUPS * 256), F32),
            pltpu.VMEM((128, 256), F32),
        ],
        1,
        3,
        16,
    )(at, q_prev.T, g, err)
    got = [around(sent[s], s) for s in (1, 2, 3)]

    k_own, *k_sent = call(
        block_kernel,
        [sds((SIDE, SIDE), BF16)] + [sds((PIECE, SIDE), BF16)] * 3,
        [pltpu.VMEM((SIDE, SIDE), F32), pltpu.VMEM((4, SIDE, SIDE), BF16)],
        1,
        1,
        16,
    )(at, after(kernel, *sent))
    acc = call(
        own_kernel, sds((ch, CELLS), F32), [pltpu.VMEM((1, SIDE, CELLS), BF16), pltpu.VMEM((3 * ch, CELLS), F32)], 0, 2, 24
    )(k_own, g)
    got[0] = after(got[0], glt, grb, acc)

    group = sds((8, 8, GROUPS * 256), F32)
    part = call(
        sketch_kernel, group, [pltpu.VMEM((40, CELLS), F32), pltpu.VMEM((8, GROUPS * 256), F32)], 0, 5, 16
    )(sent[0], *got, x)
    part, gb, gt = lax.optimization_barrier((part, gb, gt))
    glb, grt = around(gb, 1), around(gt, 3)
    part = after(exchanged(part, "xc"), glb, grt)
    part = call(total_kernel, group, (), 0, 1, 8)(part)
    glt, grb, part, *k_sent = lax.optimization_barrier((glt, grb, part, *k_sent))
    k_got = [around(v, s) for s, v in zip((1, 2, 3), k_sent, strict=True)]
    ga, go = around(glt, 1), around(grb, 3)
    part = exchanged(part, "z")
    mine = call(
        functools.partial(image_kernel, 1.0 / workers), sds((4, 8, PAY), F32), [pltpu.VMEM((40, CELLS), F32)], 0, 2, 16
    )(part, x)
    xt, xb = cut(x)
    mine, *k_got = lax.optimization_barrier((mine, *k_got, ga, go, xt, xb))[:4]
    k_mine = jnp.stack(k_got)
    k_other = lax.ppermute(k_mine, "dp", [(i, i ^ 1) for i in range(workers)])
    theirs = lax.all_to_all(mine, "chan", 0, 0, tiled=True)
    xt, xb, theirs = lax.optimization_barrier((xt, xb, theirs))
    xlt, xrb = around(xt, 1), around(xb, 3)
    xlb, xrt = around(xb, 1), around(xt, 3)
    basis, q_part = call(
        factor_kernel,
        [sds((64, 640), F32), sds((workers, 8, 128), F32)],
        [pltpu.VMEM((4, 16, 640), F32), pltpu.VMEM((4, ch, 128), F32)],
        0,
        3,
        16,
    )(theirs, err, g)
    q_got = lax.all_to_all(q_part, "dp", 0, 0, tiled=True)
    xlt, xrb = after(xlt, q_part), after(xrb, q_part)
    xa, xo = around(xlt, 1), around(xrb, 3)

    in_grad = call(
        rest_kernel,
        sds((ch, CELLS), BF16),
        [pltpu.VMEM((3, SIDE, SIDE), BF16), pltpu.VMEM((3, SIDE, CELLS), BF16), pltpu.VMEM((3 * ch, CELLS), F32)],
        1,
        9,
        44,
    )(after(at, q_got), k_mine, k_other, glt, glb, grt, grb, ga, go, acc)

    new_error, q_factor = call(
        weight_kernel,
        [sds((ch, TAPS * 640), F32), sds((ch, 4), F32)],
        [
            pltpu.VMEM((TAPS * ch, CELLS), BF16),
            pltpu.VMEM((4 * ch, CELLS), BF16),
            pltpu.VMEM((TAPS * ch, 640), F32),
            pltpu.VMEM((128, 256), F32),
        ],
        1,
        11,
        44,
    )(at, x, xlt, xlb, xrt, xrb, xa, xo, g, err, after(q_got, in_grad), basis)
    return in_grad, q_factor, new_error[None]


def solution(mesh):
    in_specs = (
        P("chan", "dp"),
        P("chan", "dp"),
        P("chan", None),
        P("dp", "chan", None),
        P("chan", None),
    )
    out_specs = (P("chan", "dp"), P("chan", None), P("dp", "chan", None))
    return jax.shard_map(
        per_device, mesh=mesh, in_specs=in_specs, out_specs=out_specs, check_vma=False
    )
```

```python
import functools

import jax
import jax.numpy as jnp
from jax import lax
from jax.experimental import pallas as pl
from jax.experimental.pallas import tpu as pltpu
from jax.sharding import PartitionSpec as P

LAT = 64
CELLS = LAT * LAT
TAPS = 9
F32 = jnp.float32
BF16 = jnp.bfloat16
NT = (((1,), (1,)), ((), ()))
NN = (((1,), (0,)), ((), ()))
HI = lax.Precision.HIGHEST
ROLLED = BF16


def tap(t):
    return t // 3 - 1, t % 3 - 1


def dot(a, b, dims):
    return lax.dot_general(a, b, dims, preferred_element_type=F32)


def split3(v):
    hi = v.astype(BF16).astype(F32)
    rest = v - hi
    mid = rest.astype(BF16).astype(F32)
    return jnp.concatenate([hi, mid, rest - mid], axis=0).astype(BF16)


def lanes(shape):
    return lax.broadcasted_iota(jnp.int32, shape, 1)


def moved(v, t, sign=1):
    da, db = (sign * d for d in tap(t))
    off = da * LAT + db
    if off == 0:
        return v
    cell = lanes(v.shape)
    row, col = cell >> 6, cell & 63
    ok = None
    if da == 1:
        ok = row >= 1
    elif da == -1:
        ok = row < LAT - 1
    if db:
        inside = col >= 1 if db == 1 else col < LAT - 1
        ok = inside if ok is None else ok & inside
    return jnp.where(ok, pltpu.roll(v, off % CELLS, 1), 0.0)


def upper(v):
    return lax.broadcasted_iota(jnp.int32, v.shape, 0) % 8 < 4


def fold(v8):
    half = CELLS // 2
    return jnp.where(upper(v8[:, :half]), v8[:, :half], v8[:, half:])


def unfold(f):
    other = pltpu.roll(f, 4, 0)
    up = upper(f)
    return jnp.concatenate([jnp.where(up, f, other), jnp.where(up, other, f)], axis=1)


FOLD = CELLS // 2
GROUPS = 5
PAY = FOLD + GROUPS * 256


def ungroup(ref, start, ch):
    return jnp.concatenate([ref[:, start + 256 * i : start + 256 * i + ch] for i in range(GROUPS)], axis=0)


def start_kernel(j_ref, qt_ref, g_ref, e_ref, o0, o1, o2, o3, qb, rows, blocks, wide):
    ch = g_ref.shape[0]
    j = j_ref[0]
    wide[...] = jnp.zeros_like(wide)
    wide[0:4, :ch] = qt_ref[...]
    wide[4:8, :ch] = qt_ref[...]
    y3 = dot(split3(wide[0:8, :ch]), g_ref[...], NN)
    y8 = y3[0:8] + y3[8:16] + y3[16:24]
    y = fold(y8)
    q = jnp.transpose(wide[...])[:ch, :]
    for r in range(4):
        qb[r] = jnp.broadcast_to(q[:, r : r + 1], (ch, 128))
    rows[...] = jnp.zeros_like(rows)
    for t in range(TAPS):
        for v in range(5):
            at = t * 640 + v * 128
            acc = [jnp.zeros((8, 128), F32) for _ in range(4)]
            for c in range(0, ch, 8):
                e = e_ref[c : c + 8, at : at + 128]
                for r in range(4):
                    acc[r] = acc[r] + e * qb[r, c : c + 8, :]
            for r in range(4):
                rows[t * 4 + r : t * 4 + r + 1, v * 128 : (v + 1) * 128] = jnp.sum(acc[r], axis=0, keepdims=True)
    for k in range(4):
        r640 = rows[...]
        if k:
            r640 = pltpu.roll(r640, 640 - k * ch, 1)
        for i in range(GROUPS):
            blocks[k, :, 256 * i : 256 * (i + 1)] = r640[8 * i : 8 * i + 8, :256]
    for s, out in enumerate((o0, o1, o2, o3)):
        out[:, :FOLD] = y
        out[:, FOLD:] = blocks[lax.rem(j + s, 4)]


def sketch_kernel(own, r1, r2, r3, x_ref, out, stack, rows):
    ch = x_ref.shape[0]
    total = own[...] + r1[...] + r2[...] + r3[...]
    y8 = unfold(total[:, :FOLD])
    up = upper(y8)
    for i in range(GROUPS):
        second = moved(y8, 2 * i + 1) if 2 * i + 1 < TAPS else jnp.zeros_like(y8)
        stack[8 * i : 8 * i + 8, :] = jnp.where(up, moved(y8, 2 * i), second)
    c3 = dot(split3(stack[...]), x_ref[...], NT)
    c = (c3[0:40] + c3[40:80] + c3[80:120]) * (1.0 / LAT)
    rows[...] = jnp.zeros_like(rows)
    for i in range(GROUPS):
        at = 256 * i
        rows[:, at : at + ch] = c[8 * i : 8 * i + 8] + total[:, FOLD + at : FOLD + at + ch]
    for k in range(out.shape[0]):
        out[k] = rows[...]


def total_kernel(got, out):
    total = got[0]
    for k in range(1, got.shape[0]):
        total = total + got[k]
    for k in range(out.shape[0]):
        out[k] = total


def image_kernel(scale, s_ref, x_ref, out, taps):
    ch = x_ref.shape[0]
    sk = s_ref[0]
    for k in range(1, s_ref.shape[0]):
        sk = sk + s_ref[k]
    sk = sk * scale
    m = jnp.concatenate([sk[:, 256 * i : 256 * i + ch] for i in range(GROUPS)], axis=0)
    u3 = dot(split3(m), x_ref[...], NN)
    taps[...] = u3[0:40] + u3[40:80] + u3[80:120]
    z8 = jnp.zeros((8, CELLS), F32)
    up = upper(z8)
    for i in range(GROUPS):
        u = taps[8 * i : 8 * i + 8, :]
        second = moved(u, 2 * i + 1, -1) if 2 * i + 1 < TAPS else jnp.zeros_like(u)
        z8 = z8 + jnp.where(up, moved(u, 2 * i, -1), second)
    z8 = z8 + pltpu.roll(z8, 4, 0)
    folded = fold(z8)
    for k in range(4):
        out[k, :, :FOLD] = folded
        out[k, :, FOLD:] = sk


def forward_substitution(low, rows):
    done = []
    for r in range(4):
        v = rows[r]
        for s in range(r):
            v = v - low[r][s] * done[s]
        done.append(v / low[r][r])
    return done


def factor_kernel(blocks, e_ref, g_ref, basis_ref, q_out, by_rank, acc_ref):
    ch = g_ref.shape[0]
    z8 = unfold(blocks[0, :, :FOLD] + blocks[1, :, :FOLD] + blocks[2, :, :FOLD] + blocks[3, :, :FOLD])
    wide = jnp.zeros((40, 640), F32)
    lane = lanes((40, 640))
    for k in range(4):
        b = jnp.concatenate([blocks[k, :, FOLD + 256 * i : FOLD + 256 * (i + 1)] for i in range(GROUPS)], axis=0)
        b = jnp.concatenate([b, jnp.zeros((40, 384), F32)], axis=1)
        if k:
            b = pltpu.roll(b, k * ch, 1)
        wide = jnp.where((lane >= k * ch) & (lane < (k + 1) * ch), b, wide)
    by_rank[...] = jnp.zeros_like(by_rank)
    for t in range(TAPS):
        for r in range(4):
            by_rank[r, t : t + 1, :] = wide[t * 4 + r : t * 4 + r + 1]
    rows = [by_rank[r] for r in range(4)]
    low = [[None] * 4 for _ in range(4)]
    for r in range(4):
        for s in range(r + 1):
            v = jnp.sum(rows[r] * rows[s], keepdims=True)
            for k in range(s):
                v = v - low[r][k] * low[s][k]
            low[r][s] = jnp.sqrt(v) if r == s else v / low[s][s]
    basis = forward_substitution(low, rows)
    for r in range(4):
        basis_ref[r * 16 : (r + 1) * 16, :] = basis[r]
    z = forward_substitution(low, [z8[r : r + 1] for r in range(4)])
    z = jnp.concatenate(z + [jnp.zeros((4, CELLS), F32)], axis=0)
    q3 = dot(split3(z), g_ref[...], NT)
    q = (q3[0:8] + q3[8:16] + q3[16:24]) * (1.0 / LAT)
    for c0 in range(0, ch, 32):
        acc = [[jnp.zeros((8, 128), F32) for _ in range(4)] for _ in range(4)]
        for t in range(TAPS):
            for v in range(5):
                at = t * 640 + v * 128
                es = [e_ref[c0 + 8 * i : c0 + 8 * i + 8, at : at + 128] for i in range(4)]
                for r in range(4):
                    b = jnp.broadcast_to(basis_ref[r * 16 + t : r * 16 + t + 1, v * 128 : (v + 1) * 128], (8, 128))
                    for i in range(4):
                        acc[i][r] = acc[i][r] + es[i] * b
        for i in range(4):
            for r in range(4):
                acc_ref[r, c0 + 8 * i : c0 + 8 * i + 8, :] = acc[i][r]
    ones = jnp.ones((8, 128), F32)
    row = lax.broadcasted_iota(jnp.int32, q.shape, 0)
    for r in range(4):
        part = lax.dot_general(ones, acc_ref[r], NT, precision=HI, preferred_element_type=F32)
        q = jnp.where(row == r, q + part, q)
    q = jnp.concatenate([q, jnp.zeros((8, 256 - ch), F32)], axis=1)
    q = jnp.where(upper(q[:, :128]), q[:, :128], pltpu.roll(q[:, 128:], 4, 0))
    for k in range(q_out.shape[0]):
        q_out[k] = q


def right_factor(got, wide, ch):
    total = got[0]
    for k in range(1, got.shape[0]):
        total = total + got[k]
    wide[...] = jnp.zeros_like(wide)
    wide[:8, :128] = total
    wide[:8, 128:] = pltpu.roll(total, 4, 0)
    return jnp.transpose(wide[...])[:ch, :4] * (1.0 / got.shape[0])


def cols_moved(v, db):
    if db == 0:
        return v
    col = lanes(v.shape) & 63
    return jnp.where(col >= 1 if db == 1 else col < LAT - 1, pltpu.roll(v, db % CELLS, 1), jnp.zeros((), v.dtype))


def rows_moved(v):
    w = pltpu.roll(v, LAT, 1)
    edge = lanes((v.shape[0], 128))
    none = jnp.zeros((), v.dtype)
    down = jnp.concatenate([jnp.where(edge < LAT, none, w[:, :128]), w[:, 128:]], axis=1)
    up = jnp.concatenate([w[:, 128:], jnp.where(edge < LAT, w[:, :128], none)], axis=1)
    return up, v, down


def weight_kernel(j_ref, x0, xlt, xlb, xrt, xrb, xa, xb, g_ref, e_ref, got, basis_ref, out, q_out, stack, xs, acc, wide):
    ch = g_ref.shape[0]
    half = ch // 2
    j = j_ref[0]
    for ref, s, first in ((x0, 0, 0), (xlt, 1, 0), (xlb, 1, half), (xrt, 3, 0), (xrb, 3, half), (xa, 2, 0), (xb, 2, half)):
        at = pl.multiple_of(lax.rem(j + 4 - s, 4) * ch + first, 16)
        xs[pl.ds(at, ref.shape[0]), :] = ref[...]

    def shifted(i, carry):
        at = pl.multiple_of(i * 16, 16)
        g = g_ref[pl.ds(at, 16), :].astype(F32)
        for b in range(3):
            for a, v in enumerate(rows_moved(cols_moved(g, b - 1).astype(ROLLED))):
                stack[pl.ds((3 * a + b) * ch + at, 16), :] = v.astype(BF16)
        return carry

    lax.fori_loop(0, ch // 16, shifted, 0)
    step = 2048
    acc[...] = dot(stack[:, :step], xs[:, :step], NT)

    def more(i, carry):
        cells = pl.ds(pl.multiple_of(i * step, step), step)
        acc[...] += dot(stack[:, cells], xs[:, cells], NT)
        return carry

    lax.fori_loop(1, CELLS // step, more, 0)
    q_out[...] = right_factor(got, wide, ch)
    for t in range(TAPS):
        for c in range(0, ch, 32):
            rows, cols = slice(c, c + 32), slice(t * 640, (t + 1) * 640)
            v = acc[t * ch + c : t * ch + c + 32, :] * (1.0 / LAT) + e_ref[rows, cols]
            for r in range(4):
                v = v - q_out[rows, r : r + 1] * basis_ref[r * 16 + t : r * 16 + t + 1, :]
            out[rows, cols] = v


SIDE = 512
PIECE = SIDE // 2


def block_kernel(at_ref, k_ref, own, p1, p2, p3, wide, blocks):
    ch = k_ref.shape[0]
    j, piece = at_ref[0], at_ref[1]
    wide[...] = jnp.zeros_like(wide)
    lane = lanes((ch, 256))
    for k in range(4):
        for a in range(3):
            for b in range(3):
                base, off = divmod(k * ch, 128)
                at = (3 * a + b) * 4 * ch + base * 128
                v = k_ref[:, at : at + 256].astype(F32)
                base, goal = divmod(b * ch, 128)
                if goal != off:
                    v = pltpu.roll(v, (goal - off) % 256, 1)
                rows, cols = slice(a * ch, (a + 1) * ch), slice(base * 128, base * 128 + 256)
                wide[rows, cols] = jnp.where((lane >= goal) & (lane < goal + ch), v, wide[rows, cols])
        blocks[k] = jnp.transpose(wide[...]).astype(BF16)
    own[...] = blocks[j]
    rows = pl.ds(pl.multiple_of(piece * PIECE, PIECE), PIECE)
    for s, out in ((1, p1), (2, p2), (3, p3)):
        out[...] = blocks[lax.rem(j + s, 4), rows, :]


def rows_stacked(refs, g3, slot):
    ch = sum(ref.shape[0] for ref in refs)
    g3[slot, 3 * ch :, :] = jnp.zeros((SIDE - 3 * ch, CELLS), BF16)
    start = 0
    for ref in refs:

        def body(i, carry, ref=ref, start=start):
            at = pl.multiple_of(i * 16, 16)
            for a, v in enumerate(rows_moved(ref[pl.ds(at, 16), :].astype(ROLLED))):
                g3[slot, pl.ds(a * ch + start + at, 16), :] = v.astype(BF16)
            return carry

        lax.fori_loop(0, ref.shape[0] // 16, body, 0)
        start += ref.shape[0]


def products(blocks, g3, v_ref):
    step = 512
    used = v_ref.shape[0]

    def body(i, carry):
        cells = pl.ds(pl.multiple_of(i * step, step), step)
        total = None
        for slot, block in enumerate(blocks):
            p = dot(block[:used, :], g3[slot, :, cells], NN)
            total = p if total is None else total + p
        v_ref[:, cells] = total
        return carry

    lax.fori_loop(0, CELLS // step, body, 0)


def collected(v_ref, at, n):
    ch = v_ref.shape[0] // 3
    v = [v_ref[pl.ds(b * ch + at, n), :] for b in range(3)]
    return v[1] + cols_moved(v[0], -1) + cols_moved(v[2], 1)


def own_kernel(k_ref, g, out, g3, v_ref):
    rows_stacked((g,), g3, 0)
    products((k_ref,), g3, v_ref)

    def body(i, carry):
        at = pl.multiple_of(i * 16, 16)
        out[pl.ds(at, 16), :] = collected(v_ref, at, 16)
        return carry

    lax.fori_loop(0, out.shape[0] // 16, body, 0)


def rest_kernel(at_ref, mine_ref, other_ref, glt, glb, grt, grb, ga, go, acc_ref, out, blocks, g3, v_ref):
    first = pl.multiple_of(at_ref[1] * PIECE, PIECE)
    second = pl.multiple_of((1 - at_ref[1]) * PIECE, PIECE)
    for s, refs in enumerate(((glt, glb), (ga, go), (grt, grb))):
        blocks[s, pl.ds(first, PIECE), :] = mine_ref[s]
        blocks[s, pl.ds(second, PIECE), :] = other_ref[s]
        rows_stacked(refs, g3, s)
    products([blocks.at[s] for s in range(3)], g3, v_ref)

    def body(i, carry):
        at = pl.multiple_of(i * 16, 16)
        rows = pl.ds(at, 16)
        out[rows, :] = (collected(v_ref, at, 16) + acc_ref[rows, :]).astype(BF16)
        return carry

    lax.fori_loop(0, out.shape[0] // 16, body, 0)


def cut_kernel(v_ref, top, bottom):
    half = top.shape[0]
    top[...] = v_ref[:half, :]
    bottom[...] = v_ref[half:, :]


def call(kernel, out_shape, scratch=(), scalars=0, inputs=0, limit=60, **kw):
    whole = pl.BlockSpec(memory_space=pltpu.VMEM)
    scalar = pl.BlockSpec(memory_space=pltpu.SMEM)
    return pl.pallas_call(
        kernel,
        out_shape=out_shape,
        in_specs=[scalar] * scalars + [whole] * inputs,
        out_specs=jax.tree.map(lambda _: whole, out_shape),
        scratch_shapes=list(scratch),
        compiler_params=pltpu.CompilerParams(vmem_limit_bytes=limit << 20),
        **kw,
    )


def around(array, s):
    return lax.ppermute(array, "chan", [(i, (i + s) % 4) for i in range(4)])


def cut(block):
    half = jax.ShapeDtypeStruct((block.shape[0] // 2, block.shape[1]), block.dtype)
    return call(cut_kernel, [half, half], (), 0, 1, 8)(block)


def after(value, *others):
    return lax.optimization_barrier((value, *others))[0]


def line_groups(axis):
    if axis == "z":
        return [[x * 16 + z * 2 + c for z in range(8)] for x in range(4) for c in range(2)]
    return [[x * 16 + z * 2 + c for x in range(4) for c in range(2)] for z in range(8)]


def exchanged(array, axis):
    return lax.all_to_all(array, "dp", 0, 0, axis_index_groups=line_groups(axis), tiled=True)


def per_device(x, g, kernel, error_in, q_prev):
    ch = x.shape[0]
    workers = lax.axis_size("dp")
    j = lax.axis_index("chan").astype(jnp.int32)
    worker = lax.axis_index("dp").astype(jnp.int32)
    at = jnp.stack([j, worker % 2])
    err = error_in[0]
    sds = jax.ShapeDtypeStruct

    gt, gb = cut(g)
    glt, grb = around(gt, 1), around(gb, 3)

    pay = sds((8, PAY), F32)
    sent = call(
        start_kernel,
        [pay] * 4,
        [
            pltpu.VMEM((4, ch, 128), F32),
            pltpu.VMEM((40, 640), F32),
            pltpu.VMEM((4, 8, GROUPS * 256), F32),
            pltpu.VMEM((128, 256), F32),
        ],
        1,
        3,
        16,
    )(at, q_prev.T, g, err)
    got = [around(sent[s], s) for s in (1, 2, 3)]

    k_own, *k_sent = call(
        block_kernel,
        [sds((SIDE, SIDE), BF16)] + [sds((PIECE, SIDE), BF16)] * 3,
        [pltpu.VMEM((SIDE, SIDE), F32), pltpu.VMEM((4, SIDE, SIDE), BF16)],
        1,
        1,
        16,
    )(at, after(kernel, *sent))
    acc = call(
        own_kernel, sds((ch, CELLS), F32), [pltpu.VMEM((1, SIDE, CELLS), BF16), pltpu.VMEM((3 * ch, CELLS), F32)], 0, 2, 24
    )(k_own, g)
    got[0] = after(got[0], glt, grb, acc)

    group = sds((8, 8, GROUPS * 256), F32)
    part = call(
        sketch_kernel, group, [pltpu.VMEM((40, CELLS), F32), pltpu.VMEM((8, GROUPS * 256), F32)], 0, 5, 16
    )(sent[0], *got, x)
    part, gb, gt = lax.optimization_barrier((part, gb, gt))
    glb, grt = around(gb, 1), around(gt, 3)
    part = after(exchanged(part, "xc"), glb, grt)
    part = call(total_kernel, group, (), 0, 1, 8)(part)
    glt, grb, part, *k_sent = lax.optimization_barrier((glt, grb, part, *k_sent))
    k_got = [around(v, s) for s, v in zip((1, 2, 3), k_sent, strict=True)]
    ga, go = around(glt, 1), around(grb, 3)
    part = exchanged(part, "z")
    mine = call(
        functools.partial(image_kernel, 1.0 / workers), sds((4, 8, PAY), F32), [pltpu.VMEM((40, CELLS), F32)], 0, 2, 16
    )(part, x)
    xt, xb = cut(x)
    mine, *k_got = lax.optimization_barrier((mine, *k_got, ga, go, xt, xb))[:4]
    k_mine = jnp.stack(k_got)
    k_other = lax.ppermute(k_mine, "dp", [(i, i ^ 1) for i in range(workers)])
    theirs = lax.all_to_all(mine, "chan", 0, 0, tiled=True)
    xt, xb, theirs = lax.optimization_barrier((xt, xb, theirs))
    xlt, xrb = around(xt, 1), around(xb, 3)
    xlb, xrt = around(xb, 1), around(xt, 3)
    basis, q_part = call(
        factor_kernel,
        [sds((64, 640), F32), sds((workers, 8, 128), F32)],
        [pltpu.VMEM((4, 16, 640), F32), pltpu.VMEM((4, ch, 128), F32)],
        0,
        3,
        16,
    )(theirs, err, g)
    q_got = lax.all_to_all(q_part, "dp", 0, 0, tiled=True)
    xlt, xrb = after(xlt, q_part), after(xrb, q_part)
    xa, xo = around(xlt, 1), around(xrb, 3)

    in_grad = call(
        rest_kernel,
        sds((ch, CELLS), BF16),
        [pltpu.VMEM((3, SIDE, SIDE), BF16), pltpu.VMEM((3, SIDE, CELLS), BF16), pltpu.VMEM((3 * ch, CELLS), F32)],
        1,
        9,
        44,
        cost_estimate=pl.CostEstimate(
            flops=2 * 3 * ch * 3 * SIDE * CELLS, transcendentals=0, bytes_accessed=12 * ch * CELLS + 12 * SIDE * SIDE
        ),
    )(after(at, q_part), k_mine, k_other, glt, glb, grt, grb, ga, go, acc)

    new_error, q_factor = call(
        weight_kernel,
        [sds((ch, TAPS * 640), F32), sds((ch, 4), F32)],
        [
            pltpu.VMEM((TAPS * ch, CELLS), BF16),
            pltpu.VMEM((4 * ch, CELLS), BF16),
            pltpu.VMEM((TAPS * ch, 640), F32),
            pltpu.VMEM((128, 256), F32),
        ],
        1,
        11,
        44,
    )(at, x, xlt, xlb, xrt, xrb, xa, xo, g, err, after(q_got, in_grad), basis)
    return in_grad, q_factor, new_error[None]


def solution(mesh):
    in_specs = (
        P("chan", "dp"),
        P("chan", "dp"),
        P("chan", None),
        P("dp", "chan", None),
        P("chan", None),
    )
    out_specs = (P("chan", "dp"), P("chan", None), P("dp", "chan", None))
    return jax.shard_map(
        per_device, mesh=mesh, in_specs=in_specs, out_specs=out_specs, check_vma=False
    )
```
